128 devices in a mesh: seq: 16 (over y, x), head: 8 (over z, core).
Axes of the slice: x: 4, y: 4, z: 4, core: 2. Of those that a mesh axis runs over, the one named last changes fastest.
Arguments:
- queries: bfloat16 [16384, 8192], P('seq', 'head'), may hold values from -6 to 6
- key_rows: bfloat16 [16384, 8192], P('seq', 'head'), may hold values from -6 to 6
- value_rows: bfloat16 [16384, 8192], P('seq', 'head')
- log_decay: float32 [64, 16384], P('head', 'seq')
- doc_start: int32 [16384], P('seq'), may hold values from 0 to 1, as said below
- gate_input: bfloat16 [16384, 8192], P('seq', 'head'), may hold values from -6 to 6
- norm_gain: float32 [8192], P('head'), may hold values from 0.1 to 1.9
- out_grad: bfloat16 [16384, 8192], P('seq', 'head'), may hold values from -6 to 6
Outputs:
- gated: bfloat16 [16384, 8192], P('seq', 'head')
- gate_grad: bfloat16 [16384, 8192], P('seq', 'head')
- query_grad: bfloat16 [16384, 8192], P('seq', 'head')
- key_grad: bfloat16 [16384, 8192], P('seq', 'head')
- value_grad: bfloat16 [16384, 8192], P('seq', 'head')
The draws below stay inside these ranges and needn't reach their ends.
Inputs may be any that keep to these rules, and one draw needn't show every extreme that they name: `doc_start`: only the first 512 and the last 512 tokens of the sequence can begin a document, and each of these two ranges holds at least one start; one document runs over all devices but the first and the last.
All inputs are finite; a program needn't handle non-finite values.
Results may differ from the reference program's by a relative error of at most 0.0062.
Values sent between devices are 32-bit elements; how exact they have to be, the bound alone decides.
A program may use at most 128 MiB of HBM per device.

```python
import math
import jax
import jax.numpy as jnp
from jax import lax

HEAD_TOTAL = 64
HD = 128
TOK_DEV = 1024
BLOCK = 512
TOKEN_TOTAL = 16384


def draw_value_rows(key, part):
    key = jax.random.fold_in(key, 7)
    random_subkeys = jax.random.split(key, 3)
    column = jnp.arange(HEAD_TOTAL * HD) // HD
    col_scale = 10.0 ** (column.astype(jnp.float32) / max(HEAD_TOTAL - 1, 1))
    sample = jnp.clip(jax.random.normal(random_subkeys[0], (TOKEN_TOTAL, HEAD_TOTAL * HD), jnp.float32), -4.0, 4.0)
    row_scale = jnp.exp(jax.random.uniform(random_subkeys[2], (TOKEN_TOTAL, 1), jnp.float32, 0.0, math.log(3.0)))
    return (sample * col_scale[None, :] * row_scale * 0.25).astype(jnp.bfloat16)


def draw_log_decay(key, part):
    key = jax.random.fold_in(key, 13)
    random_subkeys = jax.random.split(key, 8)
    fast_count = max(1, 3 * HEAD_TOTAL // 8)
    middle_count = max(1, HEAD_TOTAL // 4)
    head_rank = jax.random.permutation(random_subkeys[0], HEAD_TOTAL)[:, None]
    fast = head_rank < fast_count
    middle = (head_rank >= fast_count) & (head_rank < fast_count + middle_count)
    fast_rate = jnp.exp(jax.random.uniform(random_subkeys[1], (HEAD_TOTAL, 1), jnp.float32, math.log(1.0 / 50.0), math.log(1.0 / 30.0)))
    slow_rate = jnp.exp(jax.random.uniform(random_subkeys[2], (HEAD_TOTAL, 1), jnp.float32, math.log(0.05), math.log(0.4))) / TOKEN_TOTAL
    middle_rate = jnp.exp(jax.random.uniform(random_subkeys[7], (HEAD_TOTAL, 1), jnp.float32, math.log(0.8), math.log(2.5))) / TOK_DEV
    decay_rates = jnp.where(fast, fast_rate, jnp.where(middle, middle_rate, slow_rate))
    shards = TOKEN_TOTAL // TOK_DEV
    machine_multiplier = jnp.exp(jax.random.uniform(random_subkeys[3], (HEAD_TOTAL, shards), jnp.float32, -math.log(2.0), math.log(2.0)))
    machine_multiplier = jnp.repeat(machine_multiplier, TOK_DEV, axis=1)
    random_noise = jnp.exp(jax.random.uniform(random_subkeys[4], (HEAD_TOTAL, TOKEN_TOTAL), jnp.float32, -0.35, 0.35))
    spike_amount = jax.random.uniform(random_subkeys[5], (HEAD_TOTAL, TOKEN_TOTAL), jnp.float32) < 2.0 / TOKEN_TOTAL
    layer_depth_level = jnp.log(jax.random.uniform(random_subkeys[6], (HEAD_TOTAL, TOKEN_TOTAL), jnp.float32, 0.5, 0.8))
    return jnp.where(spike_amount, layer_depth_level, -decay_rates * machine_multiplier * random_noise).astype(jnp.float32)


def draw_doc_start(key, part):
    key = jax.random.fold_in(key, 21)
    random_subkeys = jax.random.split(key, 3)
    position = jnp.arange(TOKEN_TOTAL, dtype=jnp.int32)
    half_dev = TOK_DEV // 2
    rolls = jax.random.randint(random_subkeys[0], (TOKEN_TOTAL,), 0, TOK_DEV, dtype=jnp.int32)
    edges = (position < half_dev) | (position >= TOKEN_TOTAL - half_dev)
    scattered = edges & (rolls < 4)
    first_pick = jax.random.randint(random_subkeys[1], (), 0, half_dev, dtype=jnp.int32)
    last_pick = jax.random.randint(random_subkeys[2], (), TOKEN_TOTAL - half_dev, TOKEN_TOTAL, dtype=jnp.int32)
    chosen = scattered | (position == first_pick) | (position == last_pick)
    return chosen.astype(jnp.int32)


def steps_of(key, shape, cuts, smallest, largest):
    factor_of, own = 1.0, jax.random.fold_in(key, 6)
    for dim, parts in cuts:
        draws = jnp.exp(jax.random.uniform(jax.random.fold_in(own, dim), (parts,), jnp.float32, smallest / len(cuts), largest / len(cuts)))
        factor_of = factor_of * jnp.repeat(draws, shape[dim] // parts).reshape([-1 if axis == dim else 1 for axis in range(len(shape))])
    return factor_of


def gaussian(stream_key, dims, deviation, reach, pieces=(), kind=jnp.bfloat16):
    level = steps_of(stream_key, dims, pieces, -0.22, 0.18) if pieces else 1.0
    result = jax.random.normal(stream_key, dims, jnp.float32) * deviation * level
    return jnp.minimum(jnp.maximum(result, -reach), reach).astype(kind)


def setup_inputs(seed: int = 0) -> dict:
    streams_of = jax.random.split(jax.random.key(seed), 9)
    queries = gaussian(streams_of[0], (TOKEN_TOTAL, HEAD_TOTAL * HD), 1.0, 6.0, ((0, 16), (1, 8)))
    key_rows = gaussian(streams_of[1], (TOKEN_TOTAL, HEAD_TOTAL * HD), 1.0, 6.0, ((0, 16), (1, 8)))
    value_rows = draw_value_rows(jax.random.fold_in(streams_of[8], 71), 0)
    log_decay = draw_log_decay(jax.random.fold_in(streams_of[8], 71), 0)
    doc_start = draw_doc_start(jax.random.fold_in(streams_of[8], 71), 0)
    gate_input = gaussian(streams_of[5], (TOKEN_TOTAL, HEAD_TOTAL * HD), 1.0, 6.0, ((0, 16), (1, 8)))
    norm_gain = jnp.clip(1.0 + 0.18 * jax.random.normal(streams_of[6], (HEAD_TOTAL * HD,), jnp.float32), 0.1, 1.9)
    out_grad = gaussian(streams_of[7], (TOKEN_TOTAL, HEAD_TOTAL * HD), 1.0, 6.0, ((0, 16), (1, 8)))
    return dict(queries=queries, key_rows=key_rows, value_rows=value_rows, log_decay=log_decay, doc_start=doc_start, gate_input=gate_input, norm_gain=norm_gain, out_grad=out_grad)


epsilon = 1e-06

def block_terms(log_rates, start_flags):
    cumulative = jnp.cumsum(log_rates, axis=-1)
    doc_count = jnp.cumsum(start_flags, axis=-1, dtype=jnp.int32)
    length = start_flags.shape[-1]
    position = jnp.arange(length, dtype=jnp.int32)
    allowed = (doc_count[:, None] == doc_count[None, :]) & (position[:, None] >= position[None, :])
    difference = jnp.where(allowed[None], cumulative[:, :, None] - cumulative[:, None, :], 0.0)
    weight = jnp.where(allowed[None], jnp.exp(difference), 0.0)
    entering = jnp.where((doc_count == 0)[None], jnp.exp(cumulative), 0.0)
    last_doc = doc_count[-1]
    leaving = jnp.where((doc_count == last_doc)[None], jnp.exp(cumulative[:, -1:] - cumulative), 0.0)
    passing = jnp.where(last_doc == 0, jnp.exp(cumulative[:, -1]), 0.0)
    return (weight, entering, leaving, passing)

def reference(queries, key_rows, value_rows, log_decay, doc_start, gate_input, norm_gain, out_grad):
    block_count = TOKEN_TOTAL // BLOCK
    width = HEAD_TOTAL * HD
    query_all = queries.reshape(block_count, BLOCK, HEAD_TOTAL, HD)
    key_all = key_rows.reshape(block_count, BLOCK, HEAD_TOTAL, HD)
    value_all = value_rows.reshape(block_count, BLOCK, HEAD_TOTAL, HD)
    rate_all = log_decay.reshape(HEAD_TOTAL, block_count, BLOCK).transpose(1, 0, 2)
    start_all = doc_start.reshape(block_count, BLOCK)

    def forward_step(carried, inputs):
        query_block, key_block, value_block, rate_block, start_block = inputs
        weight, entering, leaving, passing = block_terms(rate_block, start_block)
        query_f = query_block.astype(jnp.float32)
        key_f = key_block.astype(jnp.float32)
        value_f = value_block.astype(jnp.float32)
        scores = jnp.einsum('thd,shd->hts', query_f, key_f)
        weights_bf = (scores * weight).astype(jnp.bfloat16)
        held = carried.astype(jnp.bfloat16)
        inside = jnp.einsum('hts,she->the', weights_bf.astype(jnp.float32), value_f)
        outside = jnp.einsum('thd,hde->the', query_f, held.astype(jnp.float32)) * entering.T[:, :, None]
        keyed = (key_f * leaving.T[:, :, None]).astype(jnp.bfloat16)
        local = jnp.einsum('shd,she->hde', keyed.astype(jnp.float32), value_f)
        updated = passing[:, None, None] * carried + local
        return (updated, (inside + outside, held))
    start_state = jnp.zeros((HEAD_TOTAL, HD, HD), jnp.float32)
    _, (attn_blocks, held_all) = lax.scan(forward_step, start_state, (query_all, key_all, value_all, rate_all, start_all))
    attn = attn_blocks.reshape(TOKEN_TOTAL, width)
    inverse = lax.rsqrt(lax.optimization_barrier(jnp.sum(attn * attn, axis=1)) / width + epsilon)
    sig = jax.nn.sigmoid(gate_input.astype(jnp.float32))
    normed = attn * inverse[:, None] * norm_gain[None, :]
    gated = (normed * sig).astype(jnp.bfloat16)
    grad_f = out_grad.astype(jnp.float32)
    gate_grad = (grad_f * normed * sig * (1.0 - sig)).astype(jnp.bfloat16)
    gnorm = grad_f * sig
    inner = lax.optimization_barrier(jnp.sum(gnorm * norm_gain[None, :] * attn, axis=1))
    cube = inverse * inverse * inverse
    attn_grad = (inverse[:, None] * norm_gain[None, :] * gnorm - attn * cube[:, None] * inner[:, None] / width).astype(jnp.bfloat16)
    agrad_all = attn_grad.reshape(block_count, BLOCK, HEAD_TOTAL, HD)

    def backward_step(behind, inputs):
        query_block, key_block, value_block, rate_block, start_block, agrad_block, held = inputs
        weight, entering, leaving, passing = block_terms(rate_block, start_block)
        query_f = query_block.astype(jnp.float32)
        key_f = key_block.astype(jnp.float32)
        value_f = value_block.astype(jnp.float32)
        agrad_f = agrad_block.astype(jnp.float32)
        held_f = held.astype(jnp.float32)
        scores = jnp.einsum('thd,shd->hts', query_f, key_f)
        weights_bf = (scores * weight).astype(jnp.bfloat16).astype(jnp.float32)
        dscore = (jnp.einsum('the,she->hts', agrad_f, value_f) * weight).astype(jnp.bfloat16).astype(jnp.float32)
        behind_f = behind.astype(jnp.bfloat16).astype(jnp.float32)
        qgrad = jnp.einsum('hts,shd->thd', dscore, key_f) + entering.T[:, :, None] * jnp.einsum('the,hde->thd', agrad_f, held_f)
        kgrad = jnp.einsum('hts,thd->shd', dscore, query_f) + leaving.T[:, :, None] * jnp.einsum('she,hde->shd', value_f, behind_f)
        vgrad = jnp.einsum('hts,the->she', weights_bf, agrad_f) + leaving.T[:, :, None] * jnp.einsum('shd,hde->she', key_f, behind_f)
        qkeyed = (query_f * entering.T[:, :, None]).astype(jnp.bfloat16).astype(jnp.float32)
        local = jnp.einsum('thd,the->hde', qkeyed, agrad_f)
        updated = local + passing[:, None, None] * behind
        return (updated, (qgrad.astype(jnp.bfloat16), kgrad.astype(jnp.bfloat16), vgrad.astype(jnp.bfloat16)))
    _, (qgrad_all, kgrad_all, vgrad_all) = lax.scan(backward_step, start_state, (query_all, key_all, value_all, rate_all, start_all, agrad_all, held_all), reverse=True)
    query_grad = qgrad_all.reshape(TOKEN_TOTAL, width)
    key_grad = kgrad_all.reshape(TOKEN_TOTAL, width)
    value_grad = vgrad_all.reshape(TOKEN_TOTAL, width)
    return (gated, gate_grad, query_grad, key_grad, value_grad)
```

```python
import functools

import jax
import jax.numpy as jnp
from jax import lax
from jax.experimental import pallas as pl
from jax.experimental.pallas import tpu as pltpu
from jax.sharding import PartitionSpec as P

HEAD_TOTAL = 64
HD = 128
BLOCK = 512
HALF = 256
EPSILON = 1e-06
MESH = pl.DeviceIdType.MESH
F32 = jnp.float32
BF16 = jnp.bfloat16

NN = (((1,), (0,)), ((), ()))
NT = (((1,), (1,)), ((), ()))
TN = (((0,), (0,)), ((), ()))

CUM, ENTER, LEAVE, COUNT = range(4)


def mm(a, b, dims=NN):
    return lax.dot_general(a, b, dims, preferred_element_type=F32)


def pieces(x):
    hi = x.astype(BF16).astype(F32)
    rest = x - hi
    mid = rest.astype(BF16).astype(F32)
    low = (rest - mid).astype(BF16).astype(F32)
    return hi, mid, low


def running_sum(x):
    lane = lax.broadcasted_iota(jnp.int32, x.shape, 1)
    shift = 1
    while shift < x.shape[1]:
        x = x + jnp.where(lane >= shift, pltpu.roll(x, shift, 1), 0.0)
        shift *= 2
    return x


def kernel(
    n_seq, n_head, heads, blocks,
    q_hbm, k_hbm, v_hbm, gate_hbm, og_hbm, decay_ref, doc_ref, gain_ref,
    gated_ref, ggrad_ref, qgrad_ref, kgrad_ref, vgrad_ref,
    qb, kb, vb, gateb, ogb, in_sem,
    crow, passrow, cols, mask, wbuf, pbuf, attn, gbuf, keyed, qkeyed, agrad,
    local, blocal, held, bheld, acc, norm,
    fsend, frecv, fcarry, fin, bsend, brecv, bcarry, bin_, sums,
    f1s, f1r, f2s, f2r, b1s, b1r, b2s, b2r, hs, hr,
):
    seq = lax.axis_index("seq")
    hx = lax.axis_index("head")
    width = HEAD_TOTAL * HD

    barrier = pltpu.get_barrier_semaphore()

    def greet_seq(o, _):
        pl.semaphore_signal(barrier, inc=1, device_id={"seq": lax.rem(seq + o, n_seq)}, device_id_type=MESH)
        return 0

    def greet_head(o, _):
        pl.semaphore_signal(barrier, inc=1, device_id={"head": lax.rem(hx + o, n_head)}, device_id_type=MESH)
        return 0

    lax.fori_loop(1, n_seq, greet_seq, 0)
    lax.fori_loop(1, n_head, greet_head, 0)

    pairs = ((k_hbm, kb), (v_hbm, vb), (q_hbm, qb), (gate_hbm, gateb), (og_hbm, ogb))

    def load(i, h):
        src, dst = pairs[i]
        return pltpu.make_async_copy(
            src.at[:, pl.ds(pl.multiple_of(h * HD, HD), HD)], dst.at[h], in_sem.at[i, h]
        )

    def start_kv(h, _):
        load(0, h).start()
        load(1, h).start()
        return 0

    def start_rest(h, _):
        load(2, h).start()
        load(3, h).start()
        load(4, h).start()
        return 0

    lax.fori_loop(0, heads, start_kv, 0)
    lax.fori_loop(0, heads, start_rest, 0)

    doc = doc_ref[...].astype(F32)
    per = BLOCK // HD
    for b in range(blocks):
        flags = jnp.concatenate([doc[b * per + i : b * per + i + 1, :] for i in range(per)], axis=1)
        flags = jnp.broadcast_to(flags, (heads, BLOCK))
        c = running_sum(decay_ref[:, b * BLOCK : (b + 1) * BLOCK])
        r = running_sum(flags)
        c_last = c[:, BLOCK - 1 :]
        r_last = r[:, BLOCK - 1 :]
        enter = jnp.where(r == 0.0, jnp.exp(c), 0.0)
        leave = jnp.where(r == r_last, jnp.exp(c_last - c), 0.0)
        passing = jnp.where(r_last == 0.0, jnp.exp(c_last), 0.0)
        crow[b] = c
        passrow[b] = jnp.broadcast_to(passing, (heads, HD))
        hi, mid, low = pieces(jnp.concatenate([c, enter, leave, r], axis=0))
        stacked = jnp.concatenate([hi, mid, low, jnp.zeros_like(hi)], axis=0)
        cols[b] = stacked.T.astype(BF16)

    def pick(h, *quantities):
        row = lax.broadcasted_iota(jnp.int32, (HD, HD), 0)
        live = row < 96
        out = [
            jnp.where(live & ((row & 31) == quantity * 8 + h), 1.0, 0.0).astype(BF16)
            for quantity in quantities
        ]
        return jnp.concatenate(out, axis=1) if len(out) > 1 else out[0]

    def columns(b, h, *quantities):
        both = mm(cols[b], pick(h, *quantities))
        return [both[:, i * HD : (i + 1) * HD] for i in range(len(quantities))]

    def local_states(h, _):
        load(0, h).wait()
        load(1, h).wait()
        state = None
        for b in range(blocks):
            rows = pl.ds(b * BLOCK, BLOCK)
            (leave,) = columns(b, h, LEAVE)
            key = (kb[h, rows, :].astype(F32) * leave).astype(BF16)
            keyed[h, rows, :] = key
            part = mm(key, vb[h, rows, :], TN)
            local[b, h] = part
            state = part if state is None else passrow[b, pl.ds(h, 1), :] * state + part
        total = passrow[0, pl.ds(h, 1), :]
        for b in range(1, blocks):
            total = total * passrow[b, pl.ds(h, 1), :]
        for i in range(2):
            fsend[2 * h + i, 0:64, :] = state[64 * i : 64 * i + 64, :]
            fsend[2 * h + i, 64:72, :] = jnp.broadcast_to(total, (8, HD))
        return 0

    lax.fori_loop(0, heads, local_states, 0)

    pl.semaphore_wait(barrier, n_seq - 1 + n_head - 1)

    def exchange(src, dst, s_sem, r_sem, o):
        peer = lax.rem(seq + o, n_seq)
        return pltpu.make_async_remote_copy(
            src_ref=src.at[peer], dst_ref=dst.at[seq], send_sem=s_sem.at[o], recv_sem=r_sem.at[o],
            device_id={"seq": peer}, device_id_type=MESH,
        )

    def start_all(src, dst, s_sem, r_sem):
        def go(o, _):
            exchange(src, dst, s_sem, r_sem, o).start()
            return 0

        lax.fori_loop(1, n_seq, go, 0)

    def wait_all(src, dst, s_sem, r_sem):
        def go(o, _):
            exchange(src, dst, s_sem, r_sem, o).wait()
            return 0

        lax.fori_loop(1, n_seq, go, 0)

    f1 = (fsend, frecv, f1s, f1r)
    f2 = (fcarry, fin, f2s, f2r)
    b1 = (bsend, brecv, b1s, b1r)
    b2 = (bcarry, bin_, b2s, b2r)
    start_all(*f1)

    for b in range(blocks):
        (r_col,) = columns(b, 0, COUNT)
        flags = jnp.concatenate([doc[b * per + i : b * per + i + 1, :] for i in range(per)], axis=1)
        r_row = running_sum(jnp.broadcast_to(flags, (8, BLOCK)))[0:1, :]
        for i in range(BLOCK // HD):
            t = lax.broadcasted_iota(jnp.int32, (BLOCK, HD), 0)
            j = lax.broadcasted_iota(jnp.int32, (BLOCK, HD), 1) + i * HD
            same = r_col == r_row[:, i * HD : (i + 1) * HD]
            mask[b, :, i * HD : (i + 1) * HD] = jnp.where(same & (j <= t), jnp.inf, -jnp.inf)

    tiles = [(0, 0), (1, 0), (1, 1)]

    def inside_part(h, _):
        load(2, h).wait()
        for b in range(blocks):
            rows = pl.ds(b * BLOCK, BLOCK)
            cum, enter = columns(b, h, CUM, ENTER)
            query = qb[h, rows, :]
            qkeyed[h, rows, :] = (query.astype(F32) * enter).astype(BF16)
            row = crow[b, pl.ds(h, 1), :]
            out = [None, None]
            for index, (ti, tj) in enumerate(tiles):
                t = slice(ti * HALF, (ti + 1) * HALF)
                j = slice(tj * HALF, (tj + 1) * HALF)
                score = mm(query[t], kb[h, pl.ds(b * BLOCK + tj * HALF, HALF), :], NT)
                c_t = cum[t]
                diff = jnp.concatenate([c_t, c_t], axis=1) - row[:, j]
                w = jnp.exp(jnp.minimum(diff, mask[b, t, j]))
                prob = (score * w).astype(BF16)
                wbuf[h, b, index] = w.astype(BF16)
                pbuf[h, b, index] = prob
                part = mm(prob, vb[h, pl.ds(b * BLOCK + tj * HALF, HALF), :])
                out[ti] = part if out[ti] is None else out[ti] + part
            for ti in range(2):
                attn[h, pl.ds(b * BLOCK + ti * HALF, HALF), :] = out[ti]
        return 0

    lax.fori_loop(0, heads // 2, inside_part, 0)

    wait_all(*f1)
    frecv[seq] = fsend[seq]
    fcarry[0] = jnp.zeros((64, HD), F32)

    def advance(d, _):
        fcarry[d + 1] = frecv[d, 64:65, :] * fcarry[d] + frecv[d, 0:64, :]
        return 0

    lax.fori_loop(0, n_seq - 1, advance, 0)
    start_all(*f2)
    fin[seq] = fcarry[seq]

    lax.fori_loop(heads // 2, heads, inside_part, 0)

    def gate_part(h, _):
        load(3, h).wait()
        load(4, h).wait()
        sig = jax.nn.sigmoid(gateb[h].astype(F32))
        gbuf[h] = ogb[h].astype(F32) * sig * gain_ref[pl.ds(h, 1), :]
        return 0

    lax.fori_loop(0, heads, gate_part, 0)
    acc[...] = jnp.zeros_like(acc)

    wait_all(*f2)

    def outside_part(h, _):
        carry = fin[pl.ds(2 * h, 2)].reshape(HD, HD)
        for b in range(blocks):
            rows = pl.ds(b * BLOCK, BLOCK)
            state = carry.astype(BF16)
            held[b, h] = state
            out = attn[h, rows, :] + mm(qkeyed[h, rows, :], state)
            attn[h, rows, :] = out
            acc[0, rows, :] += out * out
            acc[1, rows, :] += out * gbuf[h, rows, :]
            if b + 1 < blocks:
                carry = passrow[b, pl.ds(h, 1), :] * carry + local[b, h]
        return 0

    lax.fori_loop(0, heads, outside_part, 0)

    parts = []
    for i in range(2):
        value = acc[i]
        hi = value.astype(BF16)
        parts += [hi, (value - hi.astype(F32)).astype(BF16)]
    row = lax.broadcasted_iota(jnp.int32, (8, 4 * HD), 0)
    lane = lax.broadcasted_iota(jnp.int32, (8, 4 * HD), 1)
    chooser = jnp.where((row < 4) == (lane < 2 * HD), 1.0, 0.0).astype(BF16)
    totals = mm(chooser, jnp.concatenate(parts, axis=1), NT)
    pieces_n = totals.shape[1] // HD
    sums[hx] = jnp.concatenate(
        [totals[r : r + 1, i * HD : (i + 1) * HD] for r in (0, 4) for i in range(pieces_n)], axis=0
    )

    def head_copy(o):
        peer = lax.rem(hx + o, n_head)
        return pltpu.make_async_remote_copy(
            src_ref=sums.at[hx], dst_ref=sums.at[hx], send_sem=hs.at[o], recv_sem=hr.at[o],
            device_id={"head": peer}, device_id_type=MESH,
        )

    def head_start(o, _):
        head_copy(o).start()
        return 0

    def head_wait(o, _):
        head_copy(o).wait()
        return 0

    lax.fori_loop(1, n_head, head_start, 0)
    lax.fori_loop(1, n_head, head_wait, 0)
    both = sums[0]
    for i in range(1, n_head):
        both = both + sums[i]
    inverse = lax.rsqrt(both[0:8, :] / width + EPSILON)
    coef = inverse * inverse * inverse * both[8:16, :] / width
    hi, mid, low = pieces(jnp.concatenate([inverse, coef, jnp.zeros((16, HD), F32)], axis=0))
    turned = jnp.concatenate([hi, mid, low, jnp.zeros_like(hi)], axis=0).T.astype(BF16)
    for i in range(8):
        wide = mm(turned, pick(i, 0, 1))
        norm[0, i * HD : (i + 1) * HD, :] = wide[:, :HD]
        norm[1, i * HD : (i + 1) * HD, :] = wide[:, HD:]

    def grad_part(h, _):
        state = None
        for b in reversed(range(blocks)):
            rows = pl.ds(b * BLOCK, BLOCK)
            ag = (norm[0, rows, :] * gbuf[h, rows, :] - attn[h, rows, :] * norm[1, rows, :]).astype(BF16)
            agrad[h, rows, :] = ag
            part = mm(qkeyed[h, rows, :], ag, TN)
            blocal[b, h] = part
            state = part if state is None else part + passrow[b, pl.ds(h, 1), :] * state
        bsend[2 * h] = state[0:64, :]
        bsend[2 * h + 1] = state[64:128, :]
        return 0

    lax.fori_loop(0, heads, grad_part, 0)
    start_all(*b1)

    def back_part(h, _):
        lanes = pl.ds(pl.multiple_of(h * HD, HD), HD)
        gain = gain_ref[pl.ds(h, 1), :]
        sig = jax.nn.sigmoid(gateb[h].astype(F32))
        gate = attn[h] * norm[0] * gain * sig
        gated_ref[:, lanes] = gate.astype(BF16)
        ggrad_ref[:, lanes] = (ogb[h].astype(F32) * gate * (1.0 - sig)).astype(BF16)
        for b in range(blocks):
            rows = pl.ds(b * BLOCK, BLOCK)
            (enter,) = columns(b, h, ENTER)
            query = qb[h, rows, :]
            key = kb[h, rows, :]
            value = vb[h, rows, :]
            ag = agrad[h, rows, :]
            qg = [None, None]
            kg = [None, None]
            vg = [None, None]
            for index, (ti, tj) in enumerate(tiles):
                t = slice(ti * HALF, (ti + 1) * HALF)
                j = slice(tj * HALF, (tj + 1) * HALF)
                ds = (mm(ag[t], value[j], NT) * wbuf[h, b, index].astype(F32)).astype(BF16)
                part = mm(ds, key[j])
                qg[ti] = part if qg[ti] is None else qg[ti] + part
                part = mm(ds, query[t], TN)
                kg[tj] = part if kg[tj] is None else kg[tj] + part
                part = mm(pbuf[h, b, index], ag[t], TN)
                vg[tj] = part if vg[tj] is None else vg[tj] + part
            outside = mm(ag, held[b, h], NT) * enter
            for i in range(2):
                here = pl.ds(b * BLOCK + i * HALF, HALF)
                qgrad_ref[here, lanes] = (qg[i] + outside[i * HALF : (i + 1) * HALF]).astype(BF16)
                attn[h, here, :] = kg[i]
                gbuf[h, here, :] = vg[i]
        return 0

    lax.fori_loop(0, heads // 2, back_part, 0)

    wait_all(*b1)
    brecv[seq] = bsend[seq]
    bcarry[n_seq - 1] = jnp.zeros((64, HD), F32)

    def retreat(i, _):
        d = n_seq - 1 - i
        bcarry[d - 1] = frecv[d, 64:65, :] * bcarry[d] + brecv[d]
        return 0

    lax.fori_loop(0, n_seq - 1, retreat, 0)
    start_all(*b2)
    bin_[seq] = bcarry[seq]

    lax.fori_loop(heads // 2, heads, back_part, 0)

    wait_all(*b2)

    def final_part(h, _):
        lanes = pl.ds(pl.multiple_of(h * HD, HD), HD)
        carry = bin_[pl.ds(2 * h, 2)].reshape(HD, HD)
        for b in reversed(range(blocks)):
            rows = pl.ds(b * BLOCK, BLOCK)
            (leave,) = columns(b, h, LEAVE)
            state = carry.astype(BF16)
            kgrad_ref[rows, lanes] = (
                attn[h, rows, :] + leave * mm(vb[h, rows, :], state, NT)
            ).astype(BF16)
            vgrad_ref[rows, lanes] = (gbuf[h, rows, :] + mm(keyed[h, rows, :], state)).astype(BF16)
            if b:
                carry = blocal[b, h] + passrow[b, pl.ds(h, 1), :] * carry
        return 0

    lax.fori_loop(0, heads, final_part, 0)


def solution(mesh):
    n_seq, n_head = mesh.shape["seq"], mesh.shape["head"]

    def body(queries, key_rows, value_rows, log_decay, doc_start, gate_input, norm_gain, out_grad):
        rows, width = queries.shape
        heads = width // HD
        blocks = rows // BLOCK
        whole = pl.BlockSpec(memory_space=pltpu.VMEM)
        hbm = pl.BlockSpec(memory_space=pl.ANY)
        dma = pltpu.SemaphoreType.DMA
        big = lambda kind: pltpu.VMEM((heads, rows, HD), kind)
        seq_sems = dma((n_seq,))
        outs = pl.pallas_call(
            functools.partial(kernel, n_seq, n_head, heads, blocks),
            name="lightning",
            out_shape=[pltpu.VMEM((rows, width), BF16)] * 5,
            in_specs=[hbm] * 5 + [whole] * 3,
            out_specs=[whole] * 5,
            scratch_shapes=[
                big(BF16), big(BF16), big(BF16), big(BF16), big(BF16), dma((5, heads)),
                pltpu.VMEM((blocks, heads, BLOCK), F32),
                pltpu.VMEM((blocks, heads, HD), F32),
                pltpu.VMEM((blocks, BLOCK, HD), BF16),
                pltpu.VMEM((blocks, BLOCK, BLOCK), F32),
                pltpu.VMEM((heads, blocks, 3, HALF, HALF), BF16),
                pltpu.VMEM((heads, blocks, 3, HALF, HALF), BF16),
                big(F32), big(F32), big(BF16), big(BF16), big(BF16),
                pltpu.VMEM((blocks, heads, HD, HD), F32),
                pltpu.VMEM((blocks, heads, HD, HD), F32),
                pltpu.VMEM((blocks, heads, HD, HD), BF16),
                pltpu.VMEM((8, HD), F32),
                pltpu.VMEM((2, rows, HD), F32),
                pltpu.VMEM((2, rows, HD), F32),
                pltpu.VMEM((n_seq, 72, HD), F32),
                pltpu.VMEM((n_seq, 72, HD), F32),
                pltpu.VMEM((n_seq, 64, HD), F32),
                pltpu.VMEM((n_seq, 64, HD), F32),
                pltpu.VMEM((n_seq, 64, HD), F32),
                pltpu.VMEM((n_seq, 64, HD), F32),
                pltpu.VMEM((n_seq, 64, HD), F32),
                pltpu.VMEM((n_seq, 64, HD), F32),
                pltpu.VMEM((n_head, 16, HD), F32),
                seq_sems, seq_sems, seq_sems, seq_sems, seq_sems, seq_sems, seq_sems, seq_sems,
                dma((n_head,)), dma((n_head,)),
            ],
            compiler_params=pltpu.CompilerParams(
                collective_id=0, has_side_effects=True, vmem_limit_bytes=50 << 20
            ),
        )(
            queries, key_rows, value_rows, gate_input, out_grad, log_decay,
            doc_start.reshape(8, HD), norm_gain.reshape(8, HD),
        )
        return tuple(outs)

    block = P("seq", "head")
    return jax.shard_map(
        body,
        mesh=mesh,
        in_specs=(block, block, block, P("head", "seq"), P("seq"), block, P("head"), block),
        out_specs=(block,) * 5,
        check_vma=False,
    )
```

```python
import functools

import jax
import jax.numpy as jnp
from jax import lax
from jax.experimental import pallas as pl
from jax.experimental.pallas import tpu as pltpu
from jax.sharding import PartitionSpec as P

HEAD_TOTAL = 64
HD = 128
BLOCK = 512
HALF = 256
EPSILON = 1e-06
GROUPS = 2
SPLIT_F = 4
SPLIT_B = 4
MESH = pl.DeviceIdType.MESH
F32 = jnp.float32
BF16 = jnp.bfloat16

NN = (((1,), (0,)), ((), ()))
NT = (((1,), (1,)), ((), ()))
TN = (((0,), (0,)), ((), ()))

CUM, ENTER, LEAVE, COUNT = range(4)


def mm(a, b, dims=NN):
    return lax.dot_general(a, b, dims, preferred_element_type=F32)


def pieces(x):
    hi = x.astype(BF16).astype(F32)
    rest = x - hi
    mid = rest.astype(BF16).astype(F32)
    low = (rest - mid).astype(BF16).astype(F32)
    return hi, mid, low


def running_sum(x):
    lane = lax.broadcasted_iota(jnp.int32, x.shape, 1)
    shift = 1
    while shift < x.shape[1]:
        x = x + jnp.where(lane >= shift, pltpu.roll(x, shift, 1), 0.0)
        shift *= 2
    return x


def kernel(
    n_seq, n_head, heads, blocks, groups,
    q_hbm, k_hbm, v_hbm, gate_hbm, og_hbm, decay_hbm, doc_hbm, gain_hbm,
    gated_ref, ggrad_ref, qgrad_ref, kgrad_ref, vgrad_ref,
    qb, kb, vb, gateb, ogb, in_sem, decay_ref, doc_ref, gain_ref, small_sem,
    crow, passrow, cols, mask, wbuf, pbuf, attn, gbuf, keyed, qkeyed, agrad,
    local, blocal, held, acc, norm,
    passall, fsend, frecv, fcarry, fin, bsend, brecv, bcarry, bin_, sums,
    ps, pr, f1s, f1r, f2s, f2r, b1s, b1r, b2s, b2r, hs, hr,
):
    seq = lax.axis_index("seq")
    hx = lax.axis_index("head")
    width = HEAD_TOTAL * HD
    team = heads // groups
    band = HD // n_seq

    barrier = pltpu.get_barrier_semaphore()

    def greet_seq(o, _):
        pl.semaphore_signal(barrier, inc=1, device_id={"seq": lax.rem(seq + o, n_seq)}, device_id_type=MESH)
        return 0

    def greet_head(o, _):
        pl.semaphore_signal(barrier, inc=1, device_id={"head": lax.rem(hx + o, n_head)}, device_id_type=MESH)
        return 0

    small = [
        pltpu.make_async_copy(src, dst, small_sem.at[i])
        for i, (src, dst) in enumerate(((decay_hbm, decay_ref), (doc_hbm, doc_ref), (gain_hbm, gain_ref)))
    ]
    for copy in small:
        copy.start()
    pairs = ((k_hbm, kb), (v_hbm, vb), (q_hbm, qb), (gate_hbm, gateb), (og_hbm, ogb))

    def load(i, h):
        src, dst = pairs[i]
        return pltpu.make_async_copy(
            src.at[:, pl.ds(pl.multiple_of(h * HD, HD), HD)], dst.at[h], in_sem.at[i, h]
        )

    def start_kv(h, _):
        load(0, h).start()
        load(1, h).start()
        return 0

    def start_rest(i):
        def go(h, _):
            load(i, h).start()
            return 0

        return go

    lax.fori_loop(0, heads, start_kv, 0)
    lax.fori_loop(1, n_seq, greet_seq, 0)
    lax.fori_loop(1, n_head, greet_head, 0)
    lax.fori_loop(0, heads, start_rest(2), 0)
    lax.fori_loop(0, heads, start_rest(3), 0)
    lax.fori_loop(0, heads, start_rest(4), 0)
    for copy in small:
        copy.wait()

    doc = doc_ref[...].astype(F32)
    per = BLOCK // HD
    total = None
    for b in range(blocks):
        flags = jnp.concatenate([doc[b * per + i : b * per + i + 1, :] for i in range(per)], axis=1)
        flags = jnp.broadcast_to(flags, (heads, BLOCK))
        c = running_sum(decay_ref[:, b * BLOCK : (b + 1) * BLOCK])
        r = running_sum(flags)
        c_last = c[:, BLOCK - 1 :]
        r_last = r[:, BLOCK - 1 :]
        enter = jnp.where(r == 0.0, jnp.exp(c), 0.0)
        leave = jnp.where(r == r_last, jnp.exp(c_last - c), 0.0)
        passing = jnp.where(r_last == 0.0, jnp.exp(c_last), 0.0)
        passing = jnp.broadcast_to(passing, (heads, HD))
        crow[b] = c
        passrow[b] = passing
        total = passing if total is None else total * passing
        hi, mid, low = pieces(jnp.concatenate([c, enter, leave, r], axis=0))
        stacked = jnp.concatenate([hi, mid, low, jnp.zeros_like(hi)], axis=0)
        cols[b] = stacked.T.astype(BF16)
    passall[seq] = total

    pl.semaphore_wait(barrier, n_seq - 1 + n_head - 1)

    def pass_copy(o):
        peer = lax.rem(seq + o, n_seq)
        return pltpu.make_async_remote_copy(
            src_ref=passall.at[seq], dst_ref=passall.at[seq], send_sem=ps.at[o], recv_sem=pr.at[o],
            device_id={"seq": peer}, device_id_type=MESH,
        )

    def pass_start(o, _):
        pass_copy(o).start()
        return 0

    def pass_wait(o, _):
        pass_copy(o).wait()
        return 0

    lax.fori_loop(1, n_seq, pass_start, 0)

    def pick(h, *quantities):
        row = lax.broadcasted_iota(jnp.int32, (HD, HD), 0)
        live = row < 96
        out = [
            jnp.where(live & ((row & 31) == quantity * 8 + h), 1.0, 0.0).astype(BF16)
            for quantity in quantities
        ]
        return jnp.concatenate(out, axis=1) if len(out) > 1 else out[0]

    def columns(b, h, *quantities):
        both = mm(cols[b], pick(h, *quantities))
        return [both[:, i * HD : (i + 1) * HD] for i in range(len(quantities))]

    def exchange(g, src, dst, s_sem, r_sem, o):
        peer = lax.rem(seq + o, n_seq)
        return pltpu.make_async_remote_copy(
            src_ref=src.at[g, peer], dst_ref=dst.at[g, seq], send_sem=s_sem.at[g, o], recv_sem=r_sem.at[g, o],
            device_id={"seq": peer}, device_id_type=MESH,
        )

    def start_all(g, src, dst, s_sem, r_sem):
        def go(o, _):
            exchange(g, src, dst, s_sem, r_sem, o).start()
            return 0

        lax.fori_loop(1, n_seq, go, 0)

    def wait_all(g, src, dst, s_sem, r_sem):
        def go(o, _):
            exchange(g, src, dst, s_sem, r_sem, o).wait()
            return 0

        lax.fori_loop(1, n_seq, go, 0)

    def put_bands(ref, g, h, state):
        place = pl.ds(pl.multiple_of((h - g * team) * band, band), band)
        ref[g, :, place, :] = state.reshape(n_seq, band, HD)

    def get_bands(ref, g, h):
        place = pl.ds(pl.multiple_of((h - g * team) * band, band), band)
        return ref[g, :, place, :].reshape(HD, HD)

    def pass_bands(d, g):
        return jnp.concatenate(
            [jnp.broadcast_to(passall[d, g * team + i : g * team + i + 1, :], (band, HD)) for i in range(team)],
            axis=0,
        )

    f1 = (fsend, frecv, f1s, f1r)
    f2 = (fcarry, fin, f2s, f2r)
    b1 = (bsend, brecv, b1s, b1r)
    b2 = (bcarry, bin_, b2s, b2r)

    def local_states(g):
        def go(h, _):
            load(0, h).wait()
            load(1, h).wait()
            state = None
            for b in range(blocks):
                rows = pl.ds(b * BLOCK, BLOCK)
                (leave,) = columns(b, h, LEAVE)
                key = (kb[h, rows, :].astype(F32) * leave).astype(BF16)
                keyed[h, rows, :] = key
                part = mm(key, vb[h, rows, :], TN)
                local[b, h] = part
                state = part if state is None else passrow[b, pl.ds(h, 1), :] * state + part
            put_bands(fsend, g, h, state)
            return 0

        return go

    for g in range(groups):
        lax.fori_loop(g * team, (g + 1) * team, local_states(g), 0)
        start_all(g, *f1)

    for b in range(blocks):
        (r_col,) = columns(b, 0, COUNT)
        flags = jnp.concatenate([doc[b * per + i : b * per + i + 1, :] for i in range(per)], axis=1)
        r_row = running_sum(jnp.broadcast_to(flags, (8, BLOCK)))[0:1, :]
        for i in range(BLOCK // HD):
            t = lax.broadcasted_iota(jnp.int32, (BLOCK, HD), 0)
            j = lax.broadcasted_iota(jnp.int32, (BLOCK, HD), 1) + i * HD
            same = r_col == r_row[:, i * HD : (i + 1) * HD]
            mask[b, :, i * HD : (i + 1) * HD] = jnp.where(same & (j <= t), jnp.inf, -jnp.inf)

    tiles = [(0, 0), (1, 0), (1, 1)]

    def inside_part(h, _):
        load(2, h).wait()
        for b in range(blocks):
            rows = pl.ds(b * BLOCK, BLOCK)
            cum, enter = columns(b, h, CUM, ENTER)
            query = qb[h, rows, :]
            qkeyed[h, rows, :] = (query.astype(F32) * enter).astype(BF16)
            row = crow[b, pl.ds(h, 1), :]
            out = [None, None]
            for index, (ti, tj) in enumerate(tiles):
                t = slice(ti * HALF, (ti + 1) * HALF)
                j = slice(tj * HALF, (tj + 1) * HALF)
                score = mm(query[t], kb[h, pl.ds(b * BLOCK + tj * HALF, HALF), :], NT)
                c_t = cum[t]
                diff = jnp.concatenate([c_t, c_t], axis=1) - row[:, j]
                w = jnp.exp(jnp.minimum(diff, mask[b, t, j]))
                prob = (score * w).astype(BF16)
                wbuf[h, b, index] = w.astype(BF16)
                pbuf[h, b, index] = prob
                part = mm(prob, vb[h, pl.ds(b * BLOCK + tj * HALF, HALF), :])
                out[ti] = part if out[ti] is None else out[ti] + part
            for ti in range(2):
                attn[h, pl.ds(b * BLOCK + ti * HALF, HALF), :] = out[ti]
        return 0

    lax.fori_loop(0, SPLIT_F, inside_part, 0)

    lax.fori_loop(1, n_seq, pass_wait, 0)
    for g in range(groups):
        wait_all(g, *f1)
        frecv[g, seq] = fsend[g, seq]
        fcarry[g, 0] = jnp.zeros((team * band, HD), F32)

        def advance(d, carry):
            carry = pass_bands(d, g) * carry + frecv[g, d]
            fcarry[g, d + 1] = carry
            return carry

        lax.fori_loop(0, n_seq - 1, advance, jnp.zeros((team * band, HD), F32))
        start_all(g, *f2)
        fin[g, seq] = fcarry[g, seq]

    lax.fori_loop(SPLIT_F, heads, inside_part, 0)

    def gate_part(h, _):
        load(3, h).wait()
        load(4, h).wait()
        sig = jax.nn.sigmoid(gateb[h].astype(F32))
        gbuf[h] = ogb[h].astype(F32) * sig * gain_ref[pl.ds(h, 1), :]
        return 0

    lax.fori_loop(0, heads, gate_part, 0)
    acc[...] = jnp.zeros_like(acc)

    def outside_part(g):
        def go(h, _):
            carry = get_bands(fin, g, h)
            for b in range(blocks):
                rows = pl.ds(b * BLOCK, BLOCK)
                state = carry.astype(BF16)
                held[b, h] = state
                out = attn[h, rows, :] + mm(qkeyed[h, rows, :], state)
                attn[h, rows, :] = out
                acc[0, rows, :] += out * out
                acc[1, rows, :] += out * gbuf[h, rows, :]
                if b + 1 < blocks:
                    carry = passrow[b, pl.ds(h, 1), :] * carry + local[b, h]
            return 0

        return go

    for g in range(groups):
        wait_all(g, *f2)
        lax.fori_loop(g * team, (g + 1) * team, outside_part(g), 0, unroll=4)

    parts = []
    for i in range(2):
        value = acc[i]
        hi = value.astype(BF16)
        parts += [hi, (value - hi.astype(F32)).astype(BF16)]
    row = lax.broadcasted_iota(jnp.int32, (8, 4 * HD), 0)
    lane = lax.broadcasted_iota(jnp.int32, (8, 4 * HD), 1)
    chooser = jnp.where((row < 4) == (lane < 2 * HD), 1.0, 0.0).astype(BF16)
    totals = mm(chooser, jnp.concatenate(parts, axis=1), NT)
    pieces_n = totals.shape[1] // HD
    sums[hx] = jnp.concatenate(
        [totals[r : r + 1, i * HD : (i + 1) * HD] for r in (0, 4) for i in range(pieces_n)], axis=0
    )

    def head_copy(o):
        peer = lax.rem(hx + o, n_head)
        return pltpu.make_async_remote_copy(
            src_ref=sums.at[hx], dst_ref=sums.at[hx], send_sem=hs.at[o], recv_sem=hr.at[o],
            device_id={"head": peer}, device_id_type=MESH,
        )

    def head_start(o, _):
        head_copy(o).start()
        return 0

    def head_wait(o, _):
        head_copy(o).wait()
        return 0

    lax.fori_loop(1, n_head, head_start, 0)
    lax.fori_loop(1, n_head, head_wait, 0)
    both = sums[0]
    for i in range(1, n_head):
        both = both + sums[i]
    inverse = lax.rsqrt(both[0:8, :] / width + EPSILON)
    coef = inverse * inverse * inverse * both[8:16, :] / width
    hi, mid, low = pieces(jnp.concatenate([inverse, coef, jnp.zeros((16, HD), F32)], axis=0))
    turned = jnp.concatenate([hi, mid, low, jnp.zeros_like(hi)], axis=0).T.astype(BF16)
    for i in range(8):
        wide = mm(turned, pick(i, 0, 1))
        norm[0, i * HD : (i + 1) * HD, :] = wide[:, :HD]
        norm[1, i * HD : (i + 1) * HD, :] = wide[:, HD:]

    def grad_part(g):
        def go(h, _):
            state = None
            for b in reversed(range(blocks)):
                rows = pl.ds(b * BLOCK, BLOCK)
                ag = (norm[0, rows, :] * gbuf[h, rows, :] - attn[h, rows, :] * norm[1, rows, :]).astype(BF16)
                agrad[h, rows, :] = ag
                part = mm(qkeyed[h, rows, :], ag, TN)
                blocal[b, h] = part
                state = part if state is None else part + passrow[b, pl.ds(h, 1), :] * state
            put_bands(bsend, g, h, state)
            return 0

        return go

    for g in range(groups):
        lax.fori_loop(g * team, (g + 1) * team, grad_part(g), 0, unroll=4)
        start_all(g, *b1)

    def back_part(h, _):
        lanes = pl.ds(pl.multiple_of(h * HD, HD), HD)
        gain = gain_ref[pl.ds(h, 1), :]
        sig = jax.nn.sigmoid(gateb[h].astype(F32))
        gate = attn[h] * norm[0] * gain * sig
        gated_ref[:, lanes] = gate.astype(BF16)
        ggrad_ref[:, lanes] = (ogb[h].astype(F32) * gate * (1.0 - sig)).astype(BF16)
        for b in range(blocks):
            rows = pl.ds(b * BLOCK, BLOCK)
            (enter,) = columns(b, h, ENTER)
            query = qb[h, rows, :]
            key = kb[h, rows, :]
            value = vb[h, rows, :]
            ag = agrad[h, rows, :]
            qg = [None, None]
            kg = [None, None]
            vg = [None, None]
            for index, (ti, tj) in enumerate(tiles):
                t = slice(ti * HALF, (ti + 1) * HALF)
                j = slice(tj * HALF, (tj + 1) * HALF)
                ds = (mm(ag[t], value[j], NT) * wbuf[h, b, index].astype(F32)).astype(BF16)
                part = mm(ds, key[j])
                qg[ti] = part if qg[ti] is None else qg[ti] + part
                part = mm(ds, query[t], TN)
                kg[tj] = part if kg[tj] is None else kg[tj] + part
                part = mm(pbuf[h, b, index], ag[t], TN)
                vg[tj] = part if vg[tj] is None else vg[tj] + part
            outside = mm(ag, held[b, h], NT) * enter
            for i in range(2):
                here = pl.ds(b * BLOCK + i * HALF, HALF)
                qgrad_ref[here, lanes] = (qg[i] + outside[i * HALF : (i + 1) * HALF]).astype(BF16)
                attn[h, here, :] = kg[i]
                gbuf[h, here, :] = vg[i]
        return 0

    lax.fori_loop(0, SPLIT_B, back_part, 0)

    for g in range(groups):
        wait_all(g, *b1)
        brecv[g, seq] = bsend[g, seq]
        bcarry[g, n_seq - 1] = jnp.zeros((team * band, HD), F32)

        def retreat(i, carry):
            d = n_seq - 1 - i
            carry = pass_bands(d, g) * carry + brecv[g, d]
            bcarry[g, d - 1] = carry
            return carry

        lax.fori_loop(0, n_seq - 1, retreat, jnp.zeros((team * band, HD), F32))
        start_all(g, *b2)
        bin_[g, seq] = bcarry[g, seq]

    lax.fori_loop(SPLIT_B, heads, back_part, 0)

    def final_part(g):
        def go(h, _):
            lanes = pl.ds(pl.multiple_of(h * HD, HD), HD)
            carry = get_bands(bin_, g, h)
            for b in reversed(range(blocks)):
                rows = pl.ds(b * BLOCK, BLOCK)
                (leave,) = columns(b, h, LEAVE)
                state = carry.astype(BF16)
                kgrad_ref[rows, lanes] = (
                    attn[h, rows, :] + leave * mm(vb[h, rows, :], state, NT)
                ).astype(BF16)
                vgrad_ref[rows, lanes] = (gbuf[h, rows, :] + mm(keyed[h, rows, :], state)).astype(BF16)
                if b:
                    carry = blocal[b, h] + passrow[b, pl.ds(h, 1), :] * carry
            return 0

        return go

    for g in range(groups):
        wait_all(g, *b2)
        lax.fori_loop(g * team, (g + 1) * team, final_part(g), 0, unroll=4)


def deliver(*refs):
    count = len(refs) // 2
    sems = refs[-1]
    copies = [pltpu.make_async_copy(refs[i], refs[count + i], sems.at[i]) for i in range(count)]
    for copy in copies:
        copy.start()
    for copy in copies:
        copy.wait()


def solution(mesh):
    n_seq, n_head = mesh.shape["seq"], mesh.shape["head"]

    def body(queries, key_rows, value_rows, log_decay, doc_start, gate_input, norm_gain, out_grad):
        rows, width = queries.shape
        heads = width // HD
        blocks = rows // BLOCK
        team = heads // GROUPS
        band = HD // n_seq
        whole = pl.BlockSpec(memory_space=pltpu.VMEM)
        hbm = pl.BlockSpec(memory_space=pl.ANY)
        dma = pltpu.SemaphoreType.DMA
        big = lambda kind: pltpu.VMEM((heads, rows, HD), kind)
        states = pltpu.VMEM((GROUPS, n_seq, team * band, HD), F32)
        seq_sems = dma((GROUPS, n_seq))
        outs = pl.pallas_call(
            functools.partial(kernel, n_seq, n_head, heads, blocks, GROUPS),
            name="lightning",
            out_shape=[pltpu.VMEM((rows, width), BF16)] * 5,
            in_specs=[hbm] * 8,
            out_specs=[whole] * 5,
            scratch_shapes=[
                big(BF16), big(BF16), big(BF16), big(BF16), big(BF16), dma((5, heads)),
                pltpu.VMEM((heads, rows), F32),
                pltpu.VMEM((8, HD), jnp.int32),
                pltpu.VMEM((8, HD), F32),
                dma((3,)),
                pltpu.VMEM((blocks, heads, BLOCK), F32),
                pltpu.VMEM((blocks, heads, HD), F32),
                pltpu.VMEM((blocks, BLOCK, HD), BF16),
                pltpu.VMEM((blocks, BLOCK, BLOCK), F32),
                pltpu.VMEM((heads, blocks, 3, HALF, HALF), BF16),
                pltpu.VMEM((heads, blocks, 3, HALF, HALF), BF16),
                big(F32), big(F32), big(BF16), big(BF16), big(BF16),
                pltpu.VMEM((blocks, heads, HD, HD), F32),
                pltpu.VMEM((blocks, heads, HD, HD), F32),
                pltpu.VMEM((blocks, heads, HD, HD), BF16),
                pltpu.VMEM((2, rows, HD), F32),
                pltpu.VMEM((2, rows, HD), F32),
                pltpu.VMEM((n_seq, heads, HD), F32),
                states, states, states, states, states, states, states, states,
                pltpu.VMEM((n_head, 16, HD), F32),
                dma((n_seq,)), dma((n_seq,)),
                seq_sems, seq_sems, seq_sems, seq_sems, seq_sems, seq_sems, seq_sems, seq_sems,
                dma((n_head,)), dma((n_head,)),
            ],
            compiler_params=pltpu.CompilerParams(
                collective_id=0, has_side_effects=True, vmem_limit_bytes=50 << 20
            ),
        )(
            queries, key_rows, value_rows, gate_input, out_grad, log_decay,
            doc_start.reshape(8, HD), norm_gain.reshape(8, HD),
        )
        return tuple(
            pl.pallas_call(
                deliver,
                name="deliver",
                out_shape=[jax.ShapeDtypeStruct((rows, width), BF16)] * 5,
                in_specs=[whole] * 5,
                out_specs=[hbm] * 5,
                scratch_shapes=[dma((5,))],
                compiler_params=pltpu.CompilerParams(vmem_limit_bytes=1 << 20),
            )(*[pltpu.with_memory_space_constraint(out, pltpu.VMEM) for out in outs])
        )

    block = P("seq", "head")
    return jax.shard_map(
        body,
        mesh=mesh,
        in_specs=(block, block, block, P("head", "seq"), P("seq"), block, P("head"), block),
        out_specs=(block,) * 5,
        check_vma=False,
    )
```

```python
import functools

import jax
import jax.numpy as jnp
from jax import lax
from jax.experimental import pallas as pl
from jax.experimental.pallas import tpu as pltpu
from jax.sharding import PartitionSpec as P

HEAD_TOTAL = 64
HD = 128
BLOCK = 512
HALF = 256
EPSILON = 1e-06
GROUPS = 2
SPLIT_F = (4, 4)
SPLIT_B = (4, 4)
UNROLL = True
MESH = pl.DeviceIdType.MESH
F32 = jnp.float32
BF16 = jnp.bfloat16

NN = (((1,), (0,)), ((), ()))
NT = (((1,), (1,)), ((), ()))
TN = (((0,), (0,)), ((), ()))

CUM, ENTER, LEAVE, COUNT = range(4)


def mm(a, b, dims=NN):
    return lax.dot_general(a, b, dims, preferred_element_type=F32)


def pieces(x):
    hi = x.astype(BF16).astype(F32)
    rest = x - hi
    mid = rest.astype(BF16).astype(F32)
    low = (rest - mid).astype(BF16).astype(F32)
    return hi, mid, low


def running_sum(x):
    lane = lax.broadcasted_iota(jnp.int32, x.shape, 1)
    shift = 1
    while shift < x.shape[1]:
        x = x + jnp.where(lane >= shift, pltpu.roll(x, shift, 1), 0.0)
        shift *= 2
    return x


def kernel(
    n_seq, n_head, heads, blocks, groups,
    q_hbm, k_hbm, v_hbm, gate_hbm, og_hbm, decay_hbm, doc_hbm, gain_hbm,
    gated_ref, ggrad_ref, qgrad_ref, kgrad_ref, vgrad_ref,
    qb, kb, vb, gateb, ogb, in_sem, decay_ref, doc_ref, gain_ref, small_sem,
    crow, passrow, cols, mask, wbuf, pbuf, attn, gbuf, keyed, qkeyed, agrad,
    local, blocal, held, acc, norm,
    passall, fsend, frecv, fcarry, fin, bsend, brecv, bcarry, bin_, sums,
    ps, pr, f1s, f1r, f2s, f2r, b1s, b1r, b2s, b2r, hs, hr,
):
    seq = lax.axis_index("seq")
    hx = lax.axis_index("head")
    width = HEAD_TOTAL * HD
    team = heads // groups
    band = HD // n_seq

    barrier = pltpu.get_barrier_semaphore()

    def greet_seq(o, _):
        pl.semaphore_signal(barrier, inc=1, device_id={"seq": lax.rem(seq + o, n_seq)}, device_id_type=MESH)
        return 0

    def greet_head(o, _):
        pl.semaphore_signal(barrier, inc=1, device_id={"head": lax.rem(hx + o, n_head)}, device_id_type=MESH)
        return 0

    small = [
        pltpu.make_async_copy(src, dst, small_sem.at[i])
        for i, (src, dst) in enumerate(((decay_hbm, decay_ref), (doc_hbm, doc_ref), (gain_hbm, gain_ref)))
    ]
    for copy in small:
        copy.start()
    pairs = ((k_hbm, kb), (v_hbm, vb), (q_hbm, qb), (gate_hbm, gateb), (og_hbm, ogb))

    def load(i, h):
        src, dst = pairs[i]
        return pltpu.make_async_copy(
            src.at[:, pl.ds(pl.multiple_of(h * HD, HD), HD)], dst.at[h], in_sem.at[i, h]
        )

    def start_kv(h, _):
        load(0, h).start()
        load(1, h).start()
        return 0

    def start_rest(i):
        def go(h, _):
            load(i, h).start()
            return 0

        return go

    lax.fori_loop(0, heads, start_kv, 0)
    lax.fori_loop(1, n_seq, greet_seq, 0)
    lax.fori_loop(1, n_head, greet_head, 0)
    lax.fori_loop(0, heads, start_rest(2), 0)
    lax.fori_loop(0, heads, start_rest(3), 0)
    lax.fori_loop(0, heads, start_rest(4), 0)
    for copy in small:
        copy.wait()

    doc = doc_ref[...].astype(F32)
    per = BLOCK // HD
    total = None
    for b in range(blocks):
        flags = jnp.concatenate([doc[b * per + i : b * per + i + 1, :] for i in range(per)], axis=1)
        flags = jnp.broadcast_to(flags, (heads, BLOCK))
        c = running_sum(decay_ref[:, b * BLOCK : (b + 1) * BLOCK])
        r = running_sum(flags)
        c_last = c[:, BLOCK - 1 :]
        r_last = r[:, BLOCK - 1 :]
        enter = jnp.where(r == 0.0, jnp.exp(c), 0.0)
        leave = jnp.where(r == r_last, jnp.exp(c_last - c), 0.0)
        passing = jnp.where(r_last == 0.0, jnp.exp(c_last), 0.0)
        passing = jnp.broadcast_to(passing, (heads, HD))
        crow[b] = c
        passrow[b] = passing
        total = passing if total is None else total * passing
        hi, mid, low = pieces(jnp.concatenate([c, enter, leave, r], axis=0))
        stacked = jnp.concatenate([hi, mid, low, jnp.zeros_like(hi)], axis=0)
        cols[b] = stacked.T.astype(BF16)
    passall[seq] = total

    pl.semaphore_wait(barrier, n_seq - 1 + n_head - 1)

    def pass_copy(o):
        peer = lax.rem(seq + o, n_seq)
        return pltpu.make_async_remote_copy(
            src_ref=passall.at[seq], dst_ref=passall.at[seq], send_sem=ps.at[o], recv_sem=pr.at[o],
            device_id={"seq": peer}, device_id_type=MESH,
        )

    def pass_start(o, _):
        pass_copy(o).start()
        return 0

    def pass_wait(o, _):
        pass_copy(o).wait_recv()
        return 0

    def pass_sent(o, _):
        pass_copy(o).wait_send()
        return 0

    lax.fori_loop(1, n_seq, pass_start, 0)

    def pick(h, *quantities):
        row = lax.broadcasted_iota(jnp.int32, (HD, HD), 0)
        live = row < 96
        out = [
            jnp.where(live & ((row & 31) == quantity * 8 + h), 1.0, 0.0).astype(BF16)
            for quantity in quantities
        ]
        return jnp.concatenate(out, axis=1) if len(out) > 1 else out[0]

    def columns(b, h, *quantities):
        both = mm(cols[b], pick(h, *quantities))
        return [both[:, i * HD : (i + 1) * HD] for i in range(len(quantities))]

    def exchange(g, src, dst, s_sem, r_sem, o):
        peer = lax.rem(seq + o, n_seq)
        return pltpu.make_async_remote_copy(
            src_ref=src.at[g, peer], dst_ref=dst.at[g, seq], send_sem=s_sem.at[g, o], recv_sem=r_sem.at[g, o],
            device_id={"seq": peer}, device_id_type=MESH,
        )

    def start_all(g, src, dst, s_sem, r_sem):
        def go(o, _):
            exchange(g, src, dst, s_sem, r_sem, o).start()
            return 0

        lax.fori_loop(1, n_seq, go, 0, unroll=UNROLL)

    def wait_all(g, src, dst, s_sem, r_sem):
        def go(o, _):
            exchange(g, src, dst, s_sem, r_sem, o).wait_recv()
            return 0

        lax.fori_loop(1, n_seq, go, 0, unroll=UNROLL)

    def sent_all(g, src, dst, s_sem, r_sem):
        def go(o, _):
            exchange(g, src, dst, s_sem, r_sem, o).wait_send()
            return 0

        lax.fori_loop(1, n_seq, go, 0)

    def put_bands(ref, g, h, state):
        place = pl.ds(pl.multiple_of((h - g * team) * band, band), band)
        ref[g, :, place, :] = state.reshape(n_seq, band, HD)

    def get_bands(ref, g, h):
        place = pl.ds(pl.multiple_of((h - g * team) * band, band), band)
        return ref[g, :, place, :].reshape(HD, HD)

    def pass_bands(d, g):
        return jnp.concatenate(
            [jnp.broadcast_to(passall[d, g * team + i : g * team + i + 1, :], (band, HD)) for i in range(team)],
            axis=0,
        )

    f1 = (fsend, frecv, f1s, f1r)
    f2 = (fcarry, fin, f2s, f2r)
    b1 = (bsend, brecv, b1s, b1r)
    b2 = (bcarry, bin_, b2s, b2r)

    def local_states(g):
        def go(h, _):
            load(0, h).wait()
            load(1, h).wait()
            state = None
            for b in range(blocks):
                rows = pl.ds(b * BLOCK, BLOCK)
                (leave,) = columns(b, h, LEAVE)
                key = (kb[h, rows, :].astype(F32) * leave).astype(BF16)
                keyed[h, rows, :] = key
                part = mm(key, vb[h, rows, :], TN)
                local[b, h] = part
                state = part if state is None else passrow[b, pl.ds(h, 1), :] * state + part
            put_bands(fsend, g, h, state)
            return 0

        return go

    for g in range(groups):
        lax.fori_loop(g * team, (g + 1) * team, local_states(g), 0)
        start_all(g, *f1)

    for b in range(blocks):
        (r_col,) = columns(b, 0, COUNT)
        flags = jnp.concatenate([doc[b * per + i : b * per + i + 1, :] for i in range(per)], axis=1)
        r_row = running_sum(jnp.broadcast_to(flags, (8, BLOCK)))[0:1, :]
        for i in range(BLOCK // HD):
            t = lax.broadcasted_iota(jnp.int32, (BLOCK, HD), 0)
            j = lax.broadcasted_iota(jnp.int32, (BLOCK, HD), 1) + i * HD
            same = r_col == r_row[:, i * HD : (i + 1) * HD]
            mask[b, :, i * HD : (i + 1) * HD] = jnp.where(same & (j <= t), jnp.inf, -jnp.inf)

    tiles = [(0, 0), (1, 0), (1, 1)]

    def inside_part(h, _):
        load(2, h).wait()
        for b in range(blocks):
            rows = pl.ds(b * BLOCK, BLOCK)
            cum, enter = columns(b, h, CUM, ENTER)
            query = qb[h, rows, :]
            qkeyed[h, rows, :] = (query.astype(F32) * enter).astype(BF16)
            row = crow[b, pl.ds(h, 1), :]
            out = [None, None]
            for index, (ti, tj) in enumerate(tiles):
                t = slice(ti * HALF, (ti + 1) * HALF)
                j = slice(tj * HALF, (tj + 1) * HALF)
                score = mm(query[t], kb[h, pl.ds(b * BLOCK + tj * HALF, HALF), :], NT)
                c_t = cum[t]
                diff = jnp.concatenate([c_t, c_t], axis=1) - row[:, j]
                w = jnp.exp(jnp.minimum(diff, mask[b, t, j]))
                prob = (score * w).astype(BF16)
                wbuf[h, b, index] = w.astype(BF16)
                pbuf[h, b, index] = prob
                part = mm(prob, vb[h, pl.ds(b * BLOCK + tj * HALF, HALF), :])
                out[ti] = part if out[ti] is None else out[ti] + part
            for ti in range(2):
                attn[h, pl.ds(b * BLOCK + ti * HALF, HALF), :] = out[ti]
        return 0

    lax.fori_loop(0, SPLIT_F[0], inside_part, 0)
    lax.fori_loop(1, n_seq, pass_wait, 0)
    for g in range(groups):
        if g:
            lax.fori_loop(SPLIT_F[g - 1], SPLIT_F[g], inside_part, 0)
        wait_all(g, *f1)
        frecv[g, seq] = fsend[g, seq]
        fcarry[g, 0] = jnp.zeros((team * band, HD), F32)

        def advance(d, carry):
            carry = pass_bands(d, g) * carry + frecv[g, d]
            fcarry[g, d + 1] = carry
            return carry

        lax.fori_loop(0, n_seq - 1, advance, jnp.zeros((team * band, HD), F32))
        start_all(g, *f2)
        fin[g, seq] = fcarry[g, seq]

    lax.fori_loop(SPLIT_F[-1], heads, inside_part, 0)

    def gate_part(h, _):
        load(3, h).wait()
        load(4, h).wait()
        sig = jax.nn.sigmoid(gateb[h].astype(F32))
        gbuf[h] = ogb[h].astype(F32) * sig * gain_ref[pl.ds(h, 1), :]
        return 0

    lax.fori_loop(0, heads, gate_part, 0)
    acc[...] = jnp.zeros_like(acc)

    def outside_part(g):
        def go(h, _):
            carry = get_bands(fin, g, h)
            for b in range(blocks):
                rows = pl.ds(b * BLOCK, BLOCK)
                state = carry.astype(BF16)
                held[b, h] = state
                out = attn[h, rows, :] + mm(qkeyed[h, rows, :], state)
                attn[h, rows, :] = out
                acc[0, rows, :] += out * out
                acc[1, rows, :] += out * gbuf[h, rows, :]
                if b + 1 < blocks:
                    carry = passrow[b, pl.ds(h, 1), :] * carry + local[b, h]
            return 0

        return go

    for g in range(groups):
        wait_all(g, *f2)
        lax.fori_loop(g * team, (g + 1) * team, outside_part(g), 0, unroll=4)

    parts = []
    for i in range(2):
        value = acc[i]
        hi = value.astype(BF16)
        parts += [hi, (value - hi.astype(F32)).astype(BF16)]
    row = lax.broadcasted_iota(jnp.int32, (8, 4 * HD), 0)
    lane = lax.broadcasted_iota(jnp.int32, (8, 4 * HD), 1)
    chooser = jnp.where((row < 4) == (lane < 2 * HD), 1.0, 0.0).astype(BF16)
    totals = mm(chooser, jnp.concatenate(parts, axis=1), NT)
    pieces_n = totals.shape[1] // HD
    sums[hx] = jnp.concatenate(
        [totals[r : r + 1, i * HD : (i + 1) * HD] for r in (0, 4) for i in range(pieces_n)], axis=0
    )

    def head_copy(o):
        peer = lax.rem(hx + o, n_head)
        return pltpu.make_async_remote_copy(
            src_ref=sums.at[hx], dst_ref=sums.at[hx], send_sem=hs.at[o], recv_sem=hr.at[o],
            device_id={"head": peer}, device_id_type=MESH,
        )

    def head_start(o, _):
        head_copy(o).start()
        return 0

    def head_wait(o, _):
        head_copy(o).wait_recv()
        return 0

    def head_sent(o, _):
        head_copy(o).wait_send()
        return 0

    lax.fori_loop(1, n_head, head_start, 0, unroll=UNROLL)
    lax.fori_loop(1, n_head, head_wait, 0, unroll=UNROLL)
    both = sums[0]
    for i in range(1, n_head):
        both = both + sums[i]
    inverse = lax.rsqrt(both[0:8, :] / width + EPSILON)
    coef = inverse * inverse * inverse * both[8:16, :] / width
    hi, mid, low = pieces(jnp.concatenate([inverse, coef, jnp.zeros((16, HD), F32)], axis=0))
    turned = jnp.concatenate([hi, mid, low, jnp.zeros_like(hi)], axis=0).T.astype(BF16)
    for i in range(8):
        wide = mm(turned, pick(i, 0, 1))
        norm[0, i * HD : (i + 1) * HD, :] = wide[:, :HD]
        norm[1, i * HD : (i + 1) * HD, :] = wide[:, HD:]

    def grad_part(g):
        def go(h, _):
            state = None
            for b in reversed(range(blocks)):
                rows = pl.ds(b * BLOCK, BLOCK)
                ag = (norm[0, rows, :] * gbuf[h, rows, :] - attn[h, rows, :] * norm[1, rows, :]).astype(BF16)
                agrad[h, rows, :] = ag
                part = mm(qkeyed[h, rows, :], ag, TN)
                blocal[b, h] = part
                state = part if state is None else part + passrow[b, pl.ds(h, 1), :] * state
            put_bands(bsend, g, h, state)
            return 0

        return go

    for g in range(groups):
        lax.fori_loop(g * team, (g + 1) * team, grad_part(g), 0, unroll=4)
        start_all(g, *b1)

    vkeyed = qkeyed

    def back_part(h, _):
        lanes = pl.ds(pl.multiple_of(h * HD, HD), HD)
        gain = gain_ref[pl.ds(h, 1), :]
        sig = jax.nn.sigmoid(gateb[h].astype(F32))
        gate = attn[h] * norm[0] * gain * sig
        gated_ref[:, lanes] = gate.astype(BF16)
        ggrad_ref[:, lanes] = (ogb[h].astype(F32) * gate * (1.0 - sig)).astype(BF16)
        for b in range(blocks):
            rows = pl.ds(b * BLOCK, BLOCK)
            enter, leave = columns(b, h, ENTER, LEAVE)
            query = qb[h, rows, :]
            key = kb[h, rows, :]
            value = vb[h, rows, :]
            vkeyed[h, rows, :] = (value.astype(F32) * leave).astype(BF16)
            ag = agrad[h, rows, :]
            query_t, ag_t = query.T, ag.T
            qg = [None, None]
            kg = [None, None]
            vg = [None, None]
            for index, (ti, tj) in enumerate(tiles):
                t = slice(ti * HALF, (ti + 1) * HALF)
                j = slice(tj * HALF, (tj + 1) * HALF)
                ds = (mm(ag[t], value[j], NT) * wbuf[h, b, index].astype(F32)).astype(BF16)
                part = mm(ds, key[j])
                qg[ti] = part if qg[ti] is None else qg[ti] + part
                part = mm(query_t[:, t], ds)
                kg[tj] = part if kg[tj] is None else kg[tj] + part
                part = mm(ag_t[:, t], pbuf[h, b, index])
                vg[tj] = part if vg[tj] is None else vg[tj] + part
            outside = mm(ag, held[b, h], NT) * enter
            for i in range(2):
                here = pl.ds(b * BLOCK + i * HALF, HALF)
                qgrad_ref[here, lanes] = (qg[i] + outside[i * HALF : (i + 1) * HALF]).astype(BF16)
                attn[h, here, :] = kg[i].T
                gbuf[h, here, :] = vg[i].T
        return 0

    lax.fori_loop(0, SPLIT_B[0], back_part, 0)
    for g in range(groups):
        if g:
            lax.fori_loop(SPLIT_B[g - 1], SPLIT_B[g], back_part, 0)
        wait_all(g, *b1)
        brecv[g, seq] = bsend[g, seq]
        bcarry[g, n_seq - 1] = jnp.zeros((team * band, HD), F32)

        def retreat(i, carry):
            d = n_seq - 1 - i
            carry = pass_bands(d, g) * carry + brecv[g, d]
            bcarry[g, d - 1] = carry
            return carry

        lax.fori_loop(0, n_seq - 1, retreat, jnp.zeros((team * band, HD), F32))
        start_all(g, *b2)
        bin_[g, seq] = bcarry[g, seq]

    lax.fori_loop(SPLIT_B[-1], heads, back_part, 0)

    def final_part(g):
        def go(h, _):
            lanes = pl.ds(pl.multiple_of(h * HD, HD), HD)
            carry = get_bands(bin_, g, h)
            for b in reversed(range(blocks)):
                rows = pl.ds(b * BLOCK, BLOCK)
                state = carry.astype(BF16)
                kgrad_ref[rows, lanes] = (attn[h, rows, :] + mm(vkeyed[h, rows, :], state, NT)).astype(BF16)
                vgrad_ref[rows, lanes] = (gbuf[h, rows, :] + mm(keyed[h, rows, :], state)).astype(BF16)
                if b:
                    carry = blocal[b, h] + passrow[b, pl.ds(h, 1), :] * carry
            return 0

        return go

    for g in range(groups):
        wait_all(g, *b2)
        lax.fori_loop(g * team, (g + 1) * team, final_part(g), 0, unroll=4)

    lax.fori_loop(1, n_seq, pass_sent, 0)
    lax.fori_loop(1, n_head, head_sent, 0)
    for g in range(groups):
        for route in (f1, f2, b1, b2):
            sent_all(g, *route)


def deliver(*refs):
    count = len(refs) // 2
    sems = refs[-1]
    copies = [pltpu.make_async_copy(refs[i], refs[count + i], sems.at[i]) for i in range(count)]
    for copy in copies:
        copy.start()
    for copy in copies:
        copy.wait()


def solution(mesh):
    n_seq, n_head = mesh.shape["seq"], mesh.shape["head"]

    def body(queries, key_rows, value_rows, log_decay, doc_start, gate_input, norm_gain, out_grad):
        rows, width = queries.shape
        heads = width // HD
        blocks = rows // BLOCK
        team = heads // GROUPS
        band = HD // n_seq
        whole = pl.BlockSpec(memory_space=pltpu.VMEM)
        hbm = pl.BlockSpec(memory_space=pl.ANY)
        dma = pltpu.SemaphoreType.DMA
        big = lambda kind: pltpu.VMEM((heads, rows, HD), kind)
        states = pltpu.VMEM((GROUPS, n_seq, team * band, HD), F32)
        seq_sems = dma((GROUPS, n_seq))
        outs = pl.pallas_call(
            functools.partial(kernel, n_seq, n_head, heads, blocks, GROUPS),
            name="lightning",
            out_shape=[pltpu.VMEM((rows, width), BF16)] * 5,
            in_specs=[hbm] * 8,
            out_specs=[whole] * 5,
            scratch_shapes=[
                big(BF16), big(BF16), big(BF16), big(BF16), big(BF16), dma((5, heads)),
                pltpu.VMEM((heads, rows), F32),
                pltpu.VMEM((8, HD), jnp.int32),
                pltpu.VMEM((8, HD), F32),
                dma((3,)),
                pltpu.VMEM((blocks, heads, BLOCK), F32),
                pltpu.VMEM((blocks, heads, HD), F32),
                pltpu.VMEM((blocks, BLOCK, HD), BF16),
                pltpu.VMEM((blocks, BLOCK, BLOCK), F32),
                pltpu.VMEM((heads, blocks, 3, HALF, HALF), BF16),
                pltpu.VMEM((heads, blocks, 3, HALF, HALF), BF16),
                big(F32), big(F32), big(BF16), big(BF16), big(BF16),
                pltpu.VMEM((blocks, heads, HD, HD), F32),
                pltpu.VMEM((blocks, heads, HD, HD), F32),
                pltpu.VMEM((blocks, heads, HD, HD), BF16),
                pltpu.VMEM((2, rows, HD), F32),
                pltpu.VMEM((2, rows, HD), F32),
                pltpu.VMEM((n_seq, heads, HD), F32),
                states, states, states, states, states, states, states, states,
                pltpu.VMEM((n_head, 16, HD), F32),
                dma((n_seq,)), dma((n_seq,)),
                seq_sems, seq_sems, seq_sems, seq_sems, seq_sems, seq_sems, seq_sems, seq_sems,
                dma((n_head,)), dma((n_head,)),
            ],
            compiler_params=pltpu.CompilerParams(
                collective_id=0, has_side_effects=True, vmem_limit_bytes=50 << 20
            ),
        )(
            queries, key_rows, value_rows, gate_input, out_grad, log_decay,
            doc_start.reshape(8, HD), norm_gain.reshape(8, HD),
        )
        return tuple(
            pl.pallas_call(
                deliver,
                name="deliver",
                out_shape=[jax.ShapeDtypeStruct((rows, width), BF16)] * 5,
                in_specs=[whole] * 5,
                out_specs=[hbm] * 5,
                scratch_shapes=[dma((5,))],
                compiler_params=pltpu.CompilerParams(vmem_limit_bytes=1 << 20),
            )(*[pltpu.with_memory_space_constraint(out, pltpu.VMEM) for out in outs])
        )

    block = P("seq", "head")
    return jax.shard_map(
        body,
        mesh=mesh,
        in_specs=(block, block, block, P("head", "seq"), P("seq"), block, P("head"), block),
        out_specs=(block,) * 5,
        check_vma=False,
    )
```

```python
import functools

import jax
import jax.numpy as jnp
from jax import lax
from jax.experimental import pallas as pl
from jax.experimental.pallas import tpu as pltpu
from jax.sharding import PartitionSpec as P

HEAD_TOTAL = 64
HD = 128
BLOCK = 512
HALF = 256
EPSILON = 1e-06
GROUPS = 2
SPLIT_F = (4, 4)
SPLIT_B = (4, 4)
UNROLL = True
TEAM = 2
MESH = pl.DeviceIdType.MESH
F32 = jnp.float32
BF16 = jnp.bfloat16

NN = (((1,), (0,)), ((), ()))
NT = (((1,), (1,)), ((), ()))
TN = (((0,), (0,)), ((), ()))

CUM, ENTER, LEAVE, COUNT = range(4)


def mm(a, b, dims=NN):
    return lax.dot_general(a, b, dims, preferred_element_type=F32)


def pieces(x):
    hi = x.astype(BF16).astype(F32)
    rest = x - hi
    mid = rest.astype(BF16).astype(F32)
    low = (rest - mid).astype(BF16).astype(F32)
    return hi, mid, low


def running_sum(x):
    lane = lax.broadcasted_iota(jnp.int32, x.shape, 1)
    shift = 1
    while shift < x.shape[1]:
        x = x + jnp.where(lane >= shift, pltpu.roll(x, shift, 1), 0.0)
        shift *= 2
    return x


def kernel(
    n_seq, n_head, heads, blocks, groups,
    q_hbm, k_hbm, v_hbm, gate_hbm, og_hbm, decay_hbm, doc_hbm, gain_hbm,
    gated_ref, ggrad_ref, qgrad_ref, attn, gbuf, keyed, qkeyed, bheld,
    qb, kb, vb, gateb, ogb, in_sem, decay_ref, doc_ref, gain_ref, small_sem,
    crow, leave_rows, passrow, cols, mask, wbuf, pbuf, agrad,
    local, blocal, held, acc, norm,
    passall, fsend, frecv, fcarry, fin, bsend, brecv, bcarry, bin_, sums,
    ps, pr, f1s, f1r, f2s, f2r, b1s, b1r, b2s, b2r, hs, hr,
):
    seq = lax.axis_index("seq")
    hx = lax.axis_index("head")
    width = HEAD_TOTAL * HD
    team = heads // groups
    band = HD // n_seq

    barrier = pltpu.get_barrier_semaphore()

    def greet_seq(o, _):
        pl.semaphore_signal(barrier, inc=1, device_id={"seq": lax.rem(seq + o, n_seq)}, device_id_type=MESH)
        return 0

    def greet_head(o, _):
        pl.semaphore_signal(barrier, inc=1, device_id={"head": lax.rem(hx + o, n_head)}, device_id_type=MESH)
        return 0

    small = [
        pltpu.make_async_copy(src, dst, small_sem.at[i])
        for i, (src, dst) in enumerate(((decay_hbm, decay_ref), (doc_hbm, doc_ref), (gain_hbm, gain_ref)))
    ]
    for copy in small:
        copy.start()
    pairs = ((k_hbm, kb), (v_hbm, vb), (q_hbm, qb), (gate_hbm, gateb), (og_hbm, ogb))

    def load(i, h):
        src, dst = pairs[i]
        return pltpu.make_async_copy(
            src.at[:, pl.ds(pl.multiple_of(h * HD, HD), HD)], dst.at[h], in_sem.at[i, h]
        )

    def start_kv(h, _):
        load(0, h).start()
        load(1, h).start()
        return 0

    def start_rest(i):
        def go(h, _):
            load(i, h).start()
            return 0

        return go

    lax.fori_loop(0, heads, start_kv, 0)
    lax.fori_loop(1, n_seq, greet_seq, 0)
    lax.fori_loop(1, n_head, greet_head, 0)
    lax.fori_loop(0, heads, start_rest(2), 0)
    lax.fori_loop(0, heads, start_rest(3), 0)
    lax.fori_loop(0, heads, start_rest(4), 0)
    for copy in small:
        copy.wait()

    doc = doc_ref[...].astype(F32)
    per = BLOCK // HD
    total = None
    for b in range(blocks):
        flags = jnp.concatenate([doc[b * per + i : b * per + i + 1, :] for i in range(per)], axis=1)
        flags = jnp.broadcast_to(flags, (heads, BLOCK))
        c = running_sum(decay_ref[:, b * BLOCK : (b + 1) * BLOCK])
        r = running_sum(flags)
        c_last = c[:, BLOCK - 1 :]
        r_last = r[:, BLOCK - 1 :]
        enter = jnp.where(r == 0.0, jnp.exp(c), 0.0)
        leave = jnp.where(r == r_last, jnp.exp(c_last - c), 0.0)
        passing = jnp.where(r_last == 0.0, jnp.exp(c_last), 0.0)
        passing = jnp.broadcast_to(passing, (heads, HD))
        crow[b] = c
        leave_rows[b] = leave
        passrow[b] = passing
        total = passing if total is None else total * passing
        hi, mid, low = pieces(jnp.concatenate([c, enter, leave, r], axis=0))
        stacked = jnp.concatenate([hi, mid, low, jnp.zeros_like(hi)], axis=0)
        cols[b] = stacked.T.astype(BF16)
    passall[seq] = total

    pl.semaphore_wait(barrier, n_seq - 1 + n_head - 1)

    def pass_copy(o):
        peer = lax.rem(seq + o, n_seq)
        return pltpu.make_async_remote_copy(
            src_ref=passall.at[seq], dst_ref=passall.at[seq], send_sem=ps.at[o], recv_sem=pr.at[o],
            device_id={"seq": peer}, device_id_type=MESH,
        )

    def pass_start(o, _):
        pass_copy(o).start()
        return 0

    def pass_wait(o, _):
        pass_copy(o).wait_recv()
        return 0

    def pass_sent(o, _):
        pass_copy(o).wait_send()
        return 0

    lax.fori_loop(1, n_seq, pass_start, 0)

    def pick(h, *quantities):
        row = lax.broadcasted_iota(jnp.int32, (HD, HD), 0)
        live = row < 96
        out = [
            jnp.where(live & ((row & 31) == quantity * 8 + h), 1.0, 0.0).astype(BF16)
            for quantity in quantities
        ]
        return jnp.concatenate(out, axis=1) if len(out) > 1 else out[0]

    def columns(b, h, *quantities):
        both = mm(cols[b], pick(h, *quantities))
        return [both[:, i * HD : (i + 1) * HD] for i in range(len(quantities))]

    def exchange(g, src, dst, s_sem, r_sem, o):
        peer = lax.rem(seq + o, n_seq)
        return pltpu.make_async_remote_copy(
            src_ref=src.at[g, peer], dst_ref=dst.at[g, seq], send_sem=s_sem.at[g, o], recv_sem=r_sem.at[g, o],
            device_id={"seq": peer}, device_id_type=MESH,
        )

    def start_all(g, src, dst, s_sem, r_sem):
        def go(o, _):
            exchange(g, src, dst, s_sem, r_sem, o).start()
            return 0

        lax.fori_loop(1, n_seq, go, 0, unroll=UNROLL)

    def wait_all(g, src, dst, s_sem, r_sem):
        def go(o, _):
            exchange(g, src, dst, s_sem, r_sem, o).wait_recv()
            return 0

        lax.fori_loop(1, n_seq, go, 0, unroll=UNROLL)

    def sent_all(g, src, dst, s_sem, r_sem):
        def go(o, _):
            exchange(g, src, dst, s_sem, r_sem, o).wait_send()
            return 0

        lax.fori_loop(1, n_seq, go, 0)

    def put_bands(ref, g, h, state):
        place = pl.ds(pl.multiple_of((h - g * team) * band, band), band)
        ref[g, :, place, :] = state.reshape(n_seq, band, HD)

    def get_bands(ref, g, h):
        place = pl.ds(pl.multiple_of((h - g * team) * band, band), band)
        return ref[g, :, place, :].reshape(HD, HD)

    def pass_bands(d, g):
        return jnp.concatenate(
            [jnp.broadcast_to(passall[d, g * team + i : g * team + i + 1, :], (band, HD)) for i in range(team)],
            axis=0,
        )

    f1 = (fsend, frecv, f1s, f1r)
    f2 = (fcarry, fin, f2s, f2r)
    b1 = (bsend, brecv, b1s, b1r)
    b2 = (bcarry, bin_, b2s, b2r)

    def local_states(g):
        def go(h, _):
            load(0, h).wait()
            load(1, h).wait()
            state = None
            for b in range(blocks):
                rows = pl.ds(b * BLOCK, BLOCK)
                key_t = kb[h, rows, :].T.astype(F32) * leave_rows[b, pl.ds(h, 1), :]
                part = mm(key_t.astype(BF16), vb[h, rows, :])
                local[b, h] = part
                state = part if state is None else passrow[b, pl.ds(h, 1), :] * state + part
            put_bands(fsend, g, h, state)
            return 0

        return go

    for g in range(groups):
        lax.fori_loop(g * team, (g + 1) * team, local_states(g), 0, unroll=4)
        start_all(g, *f1)

    for b in range(blocks):
        (r_col,) = columns(b, 0, COUNT)
        flags = jnp.concatenate([doc[b * per + i : b * per + i + 1, :] for i in range(per)], axis=1)
        r_row = running_sum(jnp.broadcast_to(flags, (8, BLOCK)))[0:1, :]
        for i in range(BLOCK // HD):
            t = lax.broadcasted_iota(jnp.int32, (BLOCK, HD), 0)
            j = lax.broadcasted_iota(jnp.int32, (BLOCK, HD), 1) + i * HD
            same = r_col == r_row[:, i * HD : (i + 1) * HD]
            mask[b, :, i * HD : (i + 1) * HD] = jnp.where(same & (j <= t), jnp.inf, -jnp.inf)

    tiles = [(0, 0), (1, 0), (1, 1)]
    qkeyed_t = keyed

    def inside_part(h, _):
        load(2, h).wait()
        for b in range(blocks):
            rows = pl.ds(b * BLOCK, BLOCK)
            cum, enter = columns(b, h, CUM, ENTER)
            query = qb[h, rows, :]
            scaled = (query.astype(F32) * enter).astype(BF16)
            qkeyed[h, rows, :] = scaled
            turned = scaled.T
            for i in range(BLOCK // HD):
                qkeyed_t[h, pl.ds(b * BLOCK + i * HD, HD), :] = turned[:, i * HD : (i + 1) * HD]
            row = crow[b, pl.ds(h, 1), :]
            out = [None, None]
            for index, (ti, tj) in enumerate(tiles):
                t = slice(ti * HALF, (ti + 1) * HALF)
                j = slice(tj * HALF, (tj + 1) * HALF)
                score = mm(query[t], kb[h, pl.ds(b * BLOCK + tj * HALF, HALF), :], NT)
                c_t = cum[t]
                diff = jnp.concatenate([c_t, c_t], axis=1) - row[:, j]
                w = jnp.exp(jnp.minimum(diff, mask[b, t, j]))
                prob = (score * w).astype(BF16)
                wbuf[h, b, index] = w.astype(BF16)
                pbuf[h, b, index] = prob
                part = mm(prob, vb[h, pl.ds(b * BLOCK + tj * HALF, HALF), :])
                out[ti] = part if out[ti] is None else out[ti] + part
            for ti in range(2):
                attn[h, pl.ds(b * BLOCK + ti * HALF, HALF), :] = out[ti]
        return 0

    lax.fori_loop(0, SPLIT_F[0], inside_part, 0)
    lax.fori_loop(1, n_seq, pass_wait, 0)
    for g in range(groups):
        if g:
            lax.fori_loop(SPLIT_F[g - 1], SPLIT_F[g], inside_part, 0)
        wait_all(g, *f1)
        frecv[g, seq] = fsend[g, seq]
        fcarry[g, 0] = jnp.zeros((team * band, HD), F32)

        def advance(d, carry):
            carry = pass_bands(d, g) * carry + frecv[g, d]
            fcarry[g, d + 1] = carry
            return carry

        lax.fori_loop(0, n_seq - 1, advance, jnp.zeros((team * band, HD), F32))
        start_all(g, *f2)
        fin[g, seq] = fcarry[g, seq]

    lax.fori_loop(SPLIT_F[-1], heads, inside_part, 0)

    def gate_part(h, _):
        load(3, h).wait()
        load(4, h).wait()
        sig = jax.nn.sigmoid(gateb[h].astype(F32))
        gbuf[h] = ogb[h].astype(F32) * sig * gain_ref[pl.ds(h, 1), :]
        return 0

    lax.fori_loop(0, heads, gate_part, 0)
    acc[...] = jnp.zeros_like(acc)

    def outside_part(g):
        def go(h, _):
            carry = get_bands(fin, g, h)
            for b in range(blocks):
                rows = pl.ds(b * BLOCK, BLOCK)
                state = carry.astype(BF16)
                held[b, h] = state
                out = attn[h, rows, :] + mm(qkeyed[h, rows, :], state)
                attn[h, rows, :] = out
                acc[0, rows, :] += out * out
                acc[1, rows, :] += out * gbuf[h, rows, :]
                if b + 1 < blocks:
                    carry = passrow[b, pl.ds(h, 1), :] * carry + local[b, h]
            return 0

        return go

    for g in range(groups):
        wait_all(g, *f2)
        lax.fori_loop(g * team, (g + 1) * team, outside_part(g), 0, unroll=4)

    parts = []
    for i in range(2):
        value = acc[i]
        hi = value.astype(BF16)
        parts += [hi, (value - hi.astype(F32)).astype(BF16)]
    row = lax.broadcasted_iota(jnp.int32, (8, 4 * HD), 0)
    lane = lax.broadcasted_iota(jnp.int32, (8, 4 * HD), 1)
    chooser = jnp.where((row < 4) == (lane < 2 * HD), 1.0, 0.0).astype(BF16)
    totals = mm(chooser, jnp.concatenate(parts, axis=1), NT)
    pieces_n = totals.shape[1] // HD
    sums[hx] = jnp.concatenate(
        [totals[r : r + 1, i * HD : (i + 1) * HD] for r in (0, 4) for i in range(pieces_n)], axis=0
    )

    def head_copy(o):
        peer = lax.rem(hx + o, n_head)
        return pltpu.make_async_remote_copy(
            src_ref=sums.at[hx], dst_ref=sums.at[hx], send_sem=hs.at[o], recv_sem=hr.at[o],
            device_id={"head": peer}, device_id_type=MESH,
        )

    def head_start(o, _):
        head_copy(o).start()
        return 0

    def head_wait(o, _):
        head_copy(o).wait_recv()
        return 0

    def head_sent(o, _):
        head_copy(o).wait_send()
        return 0

    lax.fori_loop(1, n_head, head_start, 0, unroll=UNROLL)
    lax.fori_loop(1, n_head, head_wait, 0, unroll=UNROLL)
    both = sums[0]
    for i in range(1, n_head):
        both = both + sums[i]
    inverse = lax.rsqrt(both[0:8, :] / width + EPSILON)
    coef = inverse * inverse * inverse * both[8:16, :] / width
    hi, mid, low = pieces(jnp.concatenate([inverse, coef, jnp.zeros((16, HD), F32)], axis=0))
    turned = jnp.concatenate([hi, mid, low, jnp.zeros_like(hi)], axis=0).T.astype(BF16)
    for i in range(8):
        wide = mm(turned, pick(i, 0, 1))
        norm[0, i * HD : (i + 1) * HD, :] = wide[:, :HD]
        norm[1, i * HD : (i + 1) * HD, :] = wide[:, HD:]

    def grad_part(g):
        def go(h, _):
            state = None
            for b in reversed(range(blocks)):
                rows = pl.ds(b * BLOCK, BLOCK)
                ag = (norm[0, rows, :] * gbuf[h, rows, :] - attn[h, rows, :] * norm[1, rows, :]).astype(BF16)
                agrad[h, rows, :] = ag
                turned = [qkeyed_t[h, pl.ds(b * BLOCK + i * HD, HD), :] for i in range(BLOCK // HD)]
                part = mm(jnp.concatenate(turned, axis=1), ag)
                blocal[b, h] = part
                state = part if state is None else part + passrow[b, pl.ds(h, 1), :] * state
            put_bands(bsend, g, h, state)
            return 0

        return go

    for g in range(groups):
        lax.fori_loop(g * team, (g + 1) * team, grad_part(g), 0, unroll=4)
        start_all(g, *b1)

    vkeyed = qkeyed

    def back_part(h, _):
        lanes = pl.ds(pl.multiple_of(h * HD, HD), HD)
        gain = gain_ref[pl.ds(h, 1), :]
        sig = jax.nn.sigmoid(gateb[h].astype(F32))
        gate = attn[h] * norm[0] * gain * sig
        gated_ref[:, lanes] = gate.astype(BF16)
        ggrad_ref[:, lanes] = (ogb[h].astype(F32) * gate * (1.0 - sig)).astype(BF16)
        for b in range(blocks):
            rows = pl.ds(b * BLOCK, BLOCK)
            enter, leave = columns(b, h, ENTER, LEAVE)
            query = qb[h, rows, :]
            key = kb[h, rows, :]
            value = vb[h, rows, :]
            keyed[h, rows, :] = (key.astype(F32) * leave).astype(BF16)
            vkeyed[h, rows, :] = (value.astype(F32) * leave).astype(BF16)
            ag = agrad[h, rows, :]
            query_t, ag_t = query.T, ag.T
            qg = [None, None]
            kg = [None, None]
            vg = [None, None]
            for index, (ti, tj) in enumerate(tiles):
                t = slice(ti * HALF, (ti + 1) * HALF)
                j = slice(tj * HALF, (tj + 1) * HALF)
                ds = (mm(ag[t], value[j], NT) * wbuf[h, b, index].astype(F32)).astype(BF16)
                part = mm(ds, key[j])
                qg[ti] = part if qg[ti] is None else qg[ti] + part
                part = mm(query_t[:, t], ds)
                kg[tj] = part if kg[tj] is None else kg[tj] + part
                part = mm(ag_t[:, t], pbuf[h, b, index])
                vg[tj] = part if vg[tj] is None else vg[tj] + part
            outside = mm(ag, held[b, h], NT) * enter
            for i in range(2):
                here = pl.ds(b * BLOCK + i * HALF, HALF)
                qgrad_ref[here, lanes] = (qg[i] + outside[i * HALF : (i + 1) * HALF]).astype(BF16)
                attn[h, here, :] = kg[i].T
                gbuf[h, here, :] = vg[i].T
        return 0

    lax.fori_loop(0, SPLIT_B[0], back_part, 0)
    for g in range(groups):
        if g:
            lax.fori_loop(SPLIT_B[g - 1], SPLIT_B[g], back_part, 0)
        wait_all(g, *b1)
        brecv[g, seq] = bsend[g, seq]
        bcarry[g, n_seq - 1] = jnp.zeros((team * band, HD), F32)

        def retreat(i, carry):
            d = n_seq - 1 - i
            carry = pass_bands(d, g) * carry + brecv[g, d]
            bcarry[g, d - 1] = carry
            return carry

        lax.fori_loop(0, n_seq - 1, retreat, jnp.zeros((team * band, HD), F32))
        start_all(g, *b2)
        bin_[g, seq] = bcarry[g, seq]

    lax.fori_loop(SPLIT_B[-1], heads, back_part, 0)

    lax.fori_loop(1, n_seq, pass_sent, 0)
    lax.fori_loop(1, n_head, head_sent, 0)
    for g in range(groups):
        for route in (f1, f2, b1):
            sent_all(g, *route)

    def back_states(g):
        def go(h, _):
            carry = get_bands(bin_, g, h)
            for b in reversed(range(blocks)):
                bheld[b, h] = carry.astype(BF16)
                if b:
                    carry = blocal[b, h] + passrow[b, pl.ds(h, 1), :] * carry
            return 0

        return go

    for g in range(groups):
        wait_all(g, *b2)
        lax.fori_loop(g * team, (g + 1) * team, back_states(g), 0, unroll=True)
    for g in range(groups):
        sent_all(g, *b2)


def finish(
    heads, blocks,
    gated_ref, ggrad_ref, qgrad_ref, kpart, vpart, keyed, vkeyed, bheld,
    gated_hbm, ggrad_hbm, qgrad_hbm, kgrad_hbm, vgrad_hbm,
    kout, vout, sems,
):
    first = [
        pltpu.make_async_copy(src, dst, sems.at[i, 0])
        for i, (src, dst) in enumerate(
            ((gated_ref, gated_hbm), (ggrad_ref, ggrad_hbm), (qgrad_ref, qgrad_hbm))
        )
    ]
    for copy in first:
        copy.start()

    def strip(i, p):
        src, dst = ((kout, kgrad_hbm), (vout, vgrad_hbm))[i]
        lanes = pl.ds(pl.multiple_of(p * TEAM * HD, HD), TEAM * HD)
        return pltpu.make_async_copy(src.at[:, lanes], dst.at[:, lanes], sems.at[3 + i, p])

    def go(p, _):
        for i in range(TEAM):
            h = p * TEAM + i
            lanes = pl.ds(pl.multiple_of(h * HD, HD), HD)
            for b in range(blocks):
                rows = pl.ds(b * BLOCK, BLOCK)
                state = bheld[b, h]
                kout[rows, lanes] = (kpart[h, rows, :] + mm(vkeyed[h, rows, :], state, NT)).astype(BF16)
                vout[rows, lanes] = (vpart[h, rows, :] + mm(keyed[h, rows, :], state)).astype(BF16)
        strip(0, p).start()
        strip(1, p).start()
        return 0

    lax.fori_loop(0, heads // TEAM, go, 0)
    for copy in first:
        copy.wait()

    def done(p, _):
        strip(0, p).wait()
        strip(1, p).wait()
        return 0

    lax.fori_loop(0, heads // TEAM, done, 0)


def solution(mesh):
    n_seq, n_head = mesh.shape["seq"], mesh.shape["head"]

    def body(queries, key_rows, value_rows, log_decay, doc_start, gate_input, norm_gain, out_grad):
        rows, width = queries.shape
        heads = width // HD
        blocks = rows // BLOCK
        team = heads // GROUPS
        band = HD // n_seq
        whole = pl.BlockSpec(memory_space=pltpu.VMEM)
        hbm = pl.BlockSpec(memory_space=pl.ANY)
        dma = pltpu.SemaphoreType.DMA
        big = lambda kind: pltpu.VMEM((heads, rows, HD), kind)
        states = pltpu.VMEM((GROUPS, n_seq, team * band, HD), F32)
        seq_sems = dma((GROUPS, n_seq))
        outs = pl.pallas_call(
            functools.partial(kernel, n_seq, n_head, heads, blocks, GROUPS),
            name="lightning",
            out_shape=[pltpu.VMEM((rows, width), BF16)] * 3
            + [big(F32), big(F32), big(BF16), big(BF16), pltpu.VMEM((blocks, heads, HD, HD), BF16)],
            in_specs=[hbm] * 8,
            out_specs=[whole] * 8,
            scratch_shapes=[
                big(BF16), big(BF16), big(BF16), big(BF16), big(BF16), dma((5, heads)),
                pltpu.VMEM((heads, rows), F32),
                pltpu.VMEM((8, HD), jnp.int32),
                pltpu.VMEM((8, HD), F32),
                dma((3,)),
                pltpu.VMEM((blocks, heads, BLOCK), F32),
                pltpu.VMEM((blocks, heads, BLOCK), F32),
                pltpu.VMEM((blocks, heads, HD), F32),
                pltpu.VMEM((blocks, BLOCK, HD), BF16),
                pltpu.VMEM((blocks, BLOCK, BLOCK), F32),
                pltpu.VMEM((heads, blocks, 3, HALF, HALF), BF16),
                pltpu.VMEM((heads, blocks, 3, HALF, HALF), BF16),
                big(BF16),
                pltpu.VMEM((blocks, heads, HD, HD), F32),
                pltpu.VMEM((blocks, heads, HD, HD), F32),
                pltpu.VMEM((blocks, heads, HD, HD), BF16),
                pltpu.VMEM((2, rows, HD), F32),
                pltpu.VMEM((2, rows, HD), F32),
                pltpu.VMEM((n_seq, heads, HD), F32),
                states, states, states, states, states, states, states, states,
                pltpu.VMEM((n_head, 16, HD), F32),
                dma((n_seq,)), dma((n_seq,)),
                seq_sems, seq_sems, seq_sems, seq_sems, seq_sems, seq_sems, seq_sems, seq_sems,
                dma((n_head,)), dma((n_head,)),
            ],
            compiler_params=pltpu.CompilerParams(
                collective_id=0, has_side_effects=True, vmem_limit_bytes=38 << 20
            ),
        )(
            queries, key_rows, value_rows, gate_input, out_grad, log_decay,
            doc_start.reshape(8, HD), norm_gain.reshape(8, HD),
        )
        return tuple(
            pl.pallas_call(
                functools.partial(finish, heads, blocks),
                name="finish",
                out_shape=[jax.ShapeDtypeStruct((rows, width), BF16)] * 5,
                in_specs=[whole] * 8,
                out_specs=[hbm] * 5,
                scratch_shapes=[
                    pltpu.VMEM((rows, width), BF16),
                    pltpu.VMEM((rows, width), BF16),
                    dma((5, heads // TEAM)),
                ],
                compiler_params=pltpu.CompilerParams(vmem_limit_bytes=6 << 20),
            )(*[pltpu.with_memory_space_constraint(out, pltpu.VMEM) for out in outs])
        )

    block = P("seq", "head")
    return jax.shard_map(
        body,
        mesh=mesh,
        in_specs=(block, block, block, P("head", "seq"), P("seq"), block, P("head"), block),
        out_specs=(block,) * 5,
        check_vma=False,
    )
```

```python
import functools

import jax
import jax.numpy as jnp
from jax import lax
from jax.experimental import pallas as pl
from jax.experimental.pallas import tpu as pltpu
from jax.sharding import PartitionSpec as P

HEAD_TOTAL = 64
HD = 128
BLOCK = 512
HALF = 256
EPSILON = 1e-06
GROUPS = 2
SPLIT_F = (4, 4)
SPLIT_B = (4, 4)
UNROLL = True
TEAM = 2
MESH = pl.DeviceIdType.MESH
F32 = jnp.float32
BF16 = jnp.bfloat16

NN = (((1,), (0,)), ((), ()))
NT = (((1,), (1,)), ((), ()))
TN = (((0,), (0,)), ((), ()))

CUM, ENTER, LEAVE, COUNT = range(4)


def mm(a, b, dims=NN):
    return lax.dot_general(a, b, dims, preferred_element_type=F32)


def pieces(x):
    hi = x.astype(BF16).astype(F32)
    rest = x - hi
    mid = rest.astype(BF16).astype(F32)
    low = (rest - mid).astype(BF16).astype(F32)
    return hi, mid, low


def running_sum(x):
    lane = lax.broadcasted_iota(jnp.int32, x.shape, 1)
    shift = 1
    while shift < x.shape[1]:
        x = x + jnp.where(lane >= shift, pltpu.roll(x, shift, 1), 0.0)
        shift *= 2
    return x


def kernel(
    n_seq, n_head, heads, blocks, groups,
    q_hbm, k_hbm, v_hbm, gate_hbm, og_hbm, decay_hbm, doc_hbm, gain_hbm,
    gated_ref, ggrad_ref, qgrad_ref, attn, gbuf, keyed, qkeyed, bheld,
    qb, kb, vb, gateb, ogb, in_sem, decay_ref, doc_ref, gain_ref, small_sem,
    crow, leave_rows, passrow, cols, mask, wbuf, pbuf, agrad,
    local, blocal, held, acc, norm,
    fsend, frecv, fcarry, fin, bsend, brecv, bcarry, bin_, sums,
    f1s, f1r, f2s, f2r, b1s, b1r, b2s, b2r, hs, hr,
):
    seq = lax.axis_index("seq")
    hx = lax.axis_index("head")
    width = HEAD_TOTAL * HD
    team = heads // groups
    band = HD // n_seq

    barrier = pltpu.get_barrier_semaphore()

    def greet_seq(o, _):
        pl.semaphore_signal(barrier, inc=1, device_id={"seq": lax.rem(seq + o, n_seq)}, device_id_type=MESH)
        return 0

    def greet_head(o, _):
        pl.semaphore_signal(barrier, inc=1, device_id={"head": lax.rem(hx + o, n_head)}, device_id_type=MESH)
        return 0

    small = [
        pltpu.make_async_copy(src, dst, small_sem.at[i])
        for i, (src, dst) in enumerate(((decay_hbm, decay_ref), (doc_hbm, doc_ref), (gain_hbm, gain_ref)))
    ]
    for copy in small:
        copy.start()
    pairs = ((k_hbm, kb), (v_hbm, vb), (q_hbm, qb), (gate_hbm, gateb), (og_hbm, ogb))

    def load(i, h):
        src, dst = pairs[i]
        return pltpu.make_async_copy(
            src.at[:, pl.ds(pl.multiple_of(h * HD, HD), HD)], dst.at[h], in_sem.at[i, h]
        )

    def start_kv(h, _):
        load(0, h).start()
        load(1, h).start()
        return 0

    def start_rest(i):
        def go(h, _):
            load(i, h).start()
            return 0

        return go

    lax.fori_loop(0, heads, start_kv, 0)
    lax.fori_loop(1, n_seq, greet_seq, 0)
    lax.fori_loop(1, n_head, greet_head, 0)
    for copy in small:
        copy.wait()

    doc = doc_ref[...].astype(F32)
    per = BLOCK // HD
    total = None
    for b in range(blocks):
        flags = jnp.concatenate([doc[b * per + i : b * per + i + 1, :] for i in range(per)], axis=1)
        flags = jnp.broadcast_to(flags, (heads, BLOCK))
        c = running_sum(decay_ref[:, b * BLOCK : (b + 1) * BLOCK])
        r = running_sum(flags)
        c_last = c[:, BLOCK - 1 :]
        r_last = r[:, BLOCK - 1 :]
        enter = jnp.where(r == 0.0, jnp.exp(c), 0.0)
        leave = jnp.where(r == r_last, jnp.exp(c_last - c), 0.0)
        passing = jnp.where(r_last == 0.0, jnp.exp(c_last), 0.0)
        passing = jnp.broadcast_to(passing, (heads, HD))
        crow[b] = c
        leave_rows[b] = leave
        passrow[b] = passing
        total = passing if total is None else total * passing
        hi, mid, low = pieces(jnp.concatenate([c, enter, leave, r], axis=0))
        stacked = jnp.concatenate([hi, mid, low, jnp.zeros_like(hi)], axis=0)
        cols[b] = stacked.T.astype(BF16)
    tail = team * band
    fsend[0, :, tail : tail + 8, :] = jnp.broadcast_to(total[None], (n_seq, heads, HD))
    lax.fori_loop(0, heads, start_rest(2), 0)

    def pick(h, *quantities):
        row = lax.broadcasted_iota(jnp.int32, (HD, HD), 0)
        live = row < 96
        out = [
            jnp.where(live & ((row & 31) == quantity * 8 + h), 1.0, 0.0).astype(BF16)
            for quantity in quantities
        ]
        return jnp.concatenate(out, axis=1) if len(out) > 1 else out[0]

    def columns(b, h, *quantities):
        both = mm(cols[b], pick(h, *quantities))
        return [both[:, i * HD : (i + 1) * HD] for i in range(len(quantities))]

    def exchange(g, src, dst, s_sem, r_sem, o):
        peer = lax.rem(seq + o, n_seq)
        part = pl.ds(0, tail + 8 if src is fsend and g == 0 else tail)
        return pltpu.make_async_remote_copy(
            src_ref=src.at[g, peer, part], dst_ref=dst.at[g, seq, part], send_sem=s_sem.at[g, o], recv_sem=r_sem.at[g, o],
            device_id={"seq": peer}, device_id_type=MESH,
        )

    def start_all(g, src, dst, s_sem, r_sem):
        def go(o, _):
            exchange(g, src, dst, s_sem, r_sem, o).start()
            return 0

        lax.fori_loop(1, n_seq, go, 0, unroll=UNROLL)

    def wait_all(g, src, dst, s_sem, r_sem):
        def go(o, _):
            exchange(g, src, dst, s_sem, r_sem, o).wait_recv()
            return 0

        lax.fori_loop(1, n_seq, go, 0, unroll=UNROLL)

    def sent_all(g, src, dst, s_sem, r_sem):
        def go(o, _):
            exchange(g, src, dst, s_sem, r_sem, o).wait_send()
            return 0

        lax.fori_loop(1, n_seq, go, 0)

    def put_bands(ref, g, h, state):
        place = pl.ds(pl.multiple_of((h - g * team) * band, band), band)
        ref[g, :, place, :] = state.reshape(n_seq, band, HD)

    def get_bands(ref, g, h):
        place = pl.ds(pl.multiple_of((h - g * team) * band, band), band)
        return ref[g, :, place, :].reshape(HD, HD)

    def pass_bands(d, g):
        return jnp.concatenate(
            [jnp.broadcast_to(frecv[0, d, tail + g * team + i : tail + g * team + i + 1, :], (band, HD)) for i in range(team)],
            axis=0,
        )

    f1 = (fsend, frecv, f1s, f1r)
    f2 = (fcarry, fin, f2s, f2r)
    b1 = (bsend, brecv, b1s, b1r)
    b2 = (bcarry, bin_, b2s, b2r)

    def local_states(g):
        def go(h, _):
            load(0, h).wait()
            load(1, h).wait()
            state = None
            for b in range(blocks):
                rows = pl.ds(b * BLOCK, BLOCK)
                key_t = kb[h, rows, :].T.astype(F32) * leave_rows[b, pl.ds(h, 1), :]
                part = mm(key_t.astype(BF16), vb[h, rows, :])
                local[b, h] = part
                state = part if state is None else passrow[b, pl.ds(h, 1), :] * state + part
            put_bands(fsend, g, h, state)
            return 0

        return go

    for g in range(groups):
        lax.fori_loop(g * team, (g + 1) * team, local_states(g), 0, unroll=4)
        if g == 0:
            pl.semaphore_wait(barrier, n_seq - 1 + n_head - 1)
        start_all(g, *f1)
    lax.fori_loop(0, heads, start_rest(3), 0)
    lax.fori_loop(0, heads, start_rest(4), 0)

    for b in range(blocks):
        (r_col,) = columns(b, 0, COUNT)
        flags = jnp.concatenate([doc[b * per + i : b * per + i + 1, :] for i in range(per)], axis=1)
        r_row = running_sum(jnp.broadcast_to(flags, (8, BLOCK)))[0:1, :]
        for i in range(BLOCK // HD):
            t = lax.broadcasted_iota(jnp.int32, (BLOCK, HD), 0)
            j = lax.broadcasted_iota(jnp.int32, (BLOCK, HD), 1) + i * HD
            same = r_col == r_row[:, i * HD : (i + 1) * HD]
            mask[b, :, i * HD : (i + 1) * HD] = jnp.where(same & (j <= t), jnp.inf, -jnp.inf)

    tiles = [(0, 0), (1, 0), (1, 1)]
    qkeyed_t = keyed

    def inside_part(h, _):
        load(2, h).wait()
        for b in range(blocks):
            rows = pl.ds(b * BLOCK, BLOCK)
            cum, enter = columns(b, h, CUM, ENTER)
            query = qb[h, rows, :]
            scaled = (query.astype(F32) * enter).astype(BF16)
            qkeyed[h, rows, :] = scaled
            turned = scaled.T
            for i in range(BLOCK // HD):
                qkeyed_t[h, pl.ds(b * BLOCK + i * HD, HD), :] = turned[:, i * HD : (i + 1) * HD]
            row = crow[b, pl.ds(h, 1), :]
            out = [None, None]
            for index, (ti, tj) in enumerate(tiles):
                t = slice(ti * HALF, (ti + 1) * HALF)
                j = slice(tj * HALF, (tj + 1) * HALF)
                score = mm(query[t], kb[h, pl.ds(b * BLOCK + tj * HALF, HALF), :], NT)
                c_t = cum[t]
                diff = jnp.concatenate([c_t, c_t], axis=1) - row[:, j]
                w = jnp.exp(jnp.minimum(diff, mask[b, t, j]))
                prob = (score * w).astype(BF16)
                wbuf[h, b, index] = w.astype(BF16)
                pbuf[h, b, index] = prob
                part = mm(prob, vb[h, pl.ds(b * BLOCK + tj * HALF, HALF), :])
                out[ti] = part if out[ti] is None else out[ti] + part
            for ti in range(2):
                attn[h, pl.ds(b * BLOCK + ti * HALF, HALF), :] = out[ti]
        return 0

    lax.fori_loop(0, SPLIT_F[0], inside_part, 0)
    for g in range(groups):
        if g:
            lax.fori_loop(SPLIT_F[g - 1], SPLIT_F[g], inside_part, 0)
        wait_all(g, *f1)
        mine = pl.ds(0, tail + 8 if g == 0 else tail)
        frecv[g, seq, mine] = fsend[g, seq, mine]
        fcarry[g, 0] = jnp.zeros((team * band, HD), F32)

        def advance(d, carry):
            carry = pass_bands(d, g) * carry + frecv[g, d, 0:tail]
            fcarry[g, d + 1] = carry
            return carry

        lax.fori_loop(0, n_seq - 1, advance, jnp.zeros((team * band, HD), F32))
        start_all(g, *f2)
        fin[g, seq] = fcarry[g, seq]

    lax.fori_loop(SPLIT_F[-1], heads, inside_part, 0)

    def gate_part(h, _):
        load(3, h).wait()
        load(4, h).wait()
        sig = jax.nn.sigmoid(gateb[h].astype(F32))
        gbuf[h] = ogb[h].astype(F32) * sig * gain_ref[pl.ds(h, 1), :]
        return 0

    lax.fori_loop(0, heads, gate_part, 0)
    acc[...] = jnp.zeros_like(acc)

    def outside_part(g):
        def go(h, _):
            carry = get_bands(fin, g, h)
            for b in range(blocks):
                rows = pl.ds(b * BLOCK, BLOCK)
                state = carry.astype(BF16)
                held[b, h] = state
                out = attn[h, rows, :] + mm(qkeyed[h, rows, :], state)
                attn[h, rows, :] = out
                acc[0, rows, :] += out * out
                acc[1, rows, :] += out * gbuf[h, rows, :]
                if b + 1 < blocks:
                    carry = passrow[b, pl.ds(h, 1), :] * carry + local[b, h]
            return 0

        return go

    for g in range(groups):
        wait_all(g, *f2)
        lax.fori_loop(g * team, (g + 1) * team, outside_part(g), 0, unroll=4)

    parts = []
    for i in range(2):
        value = acc[i]
        hi = value.astype(BF16)
        parts += [hi, (value - hi.astype(F32)).astype(BF16)]
    row = lax.broadcasted_iota(jnp.int32, (8, 4 * HD), 0)
    lane = lax.broadcasted_iota(jnp.int32, (8, 4 * HD), 1)
    chooser = jnp.where((row < 4) == (lane < 2 * HD), 1.0, 0.0).astype(BF16)
    totals = mm(chooser, jnp.concatenate(parts, axis=1), NT)
    pieces_n = totals.shape[1] // HD
    sums[hx] = jnp.concatenate(
        [totals[r : r + 1, i * HD : (i + 1) * HD] for r in (0, 4) for i in range(pieces_n)], axis=0
    )

    def head_copy(o):
        peer = lax.rem(hx + o, n_head)
        return pltpu.make_async_remote_copy(
            src_ref=sums.at[hx], dst_ref=sums.at[hx], send_sem=hs.at[o], recv_sem=hr.at[o],
            device_id={"head": peer}, device_id_type=MESH,
        )

    def head_start(o, _):
        head_copy(o).start()
        return 0

    def head_wait(o, _):
        head_copy(o).wait_recv()
        return 0

    def head_sent(o, _):
        head_copy(o).wait_send()
        return 0

    lax.fori_loop(1, n_head, head_start, 0, unroll=UNROLL)
    lax.fori_loop(1, n_head, head_wait, 0, unroll=UNROLL)
    both = sums[0]
    for i in range(1, n_head):
        both = both + sums[i]
    inverse = lax.rsqrt(both[0:8, :] / width + EPSILON)
    coef = inverse * inverse * inverse * both[8:16, :] / width
    hi, mid, low = pieces(jnp.concatenate([inverse, coef, jnp.zeros((16, HD), F32)], axis=0))
    turned = jnp.concatenate([hi, mid, low, jnp.zeros_like(hi)], axis=0).T.astype(BF16)
    for i in range(8):
        wide = mm(turned, pick(i, 0, 1))
        norm[0, i * HD : (i + 1) * HD, :] = wide[:, :HD]
        norm[1, i * HD : (i + 1) * HD, :] = wide[:, HD:]

    def grad_part(g):
        def go(h, _):
            state = None
            for b in reversed(range(blocks)):
                rows = pl.ds(b * BLOCK, BLOCK)
                ag = (norm[0, rows, :] * gbuf[h, rows, :] - attn[h, rows, :] * norm[1, rows, :]).astype(BF16)
                agrad[h, rows, :] = ag
                turned = [qkeyed_t[h, pl.ds(b * BLOCK + i * HD, HD), :] for i in range(BLOCK // HD)]
                part = mm(jnp.concatenate(turned, axis=1), ag)
                blocal[b, h] = part
                state = part if state is None else part + passrow[b, pl.ds(h, 1), :] * state
            put_bands(bsend, g, h, state)
            return 0

        return go

    for g in range(groups):
        lax.fori_loop(g * team, (g + 1) * team, grad_part(g), 0, unroll=4)
        start_all(g, *b1)

    vkeyed = qkeyed

    def back_part(h, _):
        lanes = pl.ds(pl.multiple_of(h * HD, HD), HD)
        gain = gain_ref[pl.ds(h, 1), :]
        sig = jax.nn.sigmoid(gateb[h].astype(F32))
        gate = attn[h] * norm[0] * gain * sig
        gated_ref[:, lanes] = gate.astype(BF16)
        ggrad_ref[:, lanes] = (ogb[h].astype(F32) * gate * (1.0 - sig)).astype(BF16)
        for b in range(blocks):
            rows = pl.ds(b * BLOCK, BLOCK)
            enter, leave = columns(b, h, ENTER, LEAVE)
            query = qb[h, rows, :]
            key = kb[h, rows, :]
            value = vb[h, rows, :]
            keyed[h, rows, :] = (key.astype(F32) * leave).astype(BF16)
            vkeyed[h, rows, :] = (value.astype(F32) * leave).astype(BF16)
            ag = agrad[h, rows, :]
            query_t, ag_t = query.T, ag.T
            qg = [None, None]
            kg = [None, None]
            vg = [None, None]
            for index, (ti, tj) in enumerate(tiles):
                t = slice(ti * HALF, (ti + 1) * HALF)
                j = slice(tj * HALF, (tj + 1) * HALF)
                ds = (mm(ag[t], value[j], NT) * wbuf[h, b, index].astype(F32)).astype(BF16)
                part = mm(ds, key[j])
                qg[ti] = part if qg[ti] is None else qg[ti] + part
                part = mm(query_t[:, t], ds)
                kg[tj] = part if kg[tj] is None else kg[tj] + part
                part = mm(ag_t[:, t], pbuf[h, b, index])
                vg[tj] = part if vg[tj] is None else vg[tj] + part
            outside = mm(ag, held[b, h], NT) * enter
            for i in range(2):
                here = pl.ds(b * BLOCK + i * HALF, HALF)
                qgrad_ref[here, lanes] = (qg[i] + outside[i * HALF : (i + 1) * HALF]).astype(BF16)
                attn[h, here, :] = kg[i].T
                gbuf[h, here, :] = vg[i].T
        return 0

    lax.fori_loop(0, SPLIT_B[0], back_part, 0)
    for g in range(groups):
        if g:
            lax.fori_loop(SPLIT_B[g - 1], SPLIT_B[g], back_part, 0)
        wait_all(g, *b1)
        brecv[g, seq] = bsend[g, seq]
        bcarry[g, n_seq - 1] = jnp.zeros((team * band, HD), F32)

        def retreat(i, carry):
            d = n_seq - 1 - i
            carry = pass_bands(d, g) * carry + brecv[g, d]
            bcarry[g, d - 1] = carry
            return carry

        lax.fori_loop(0, n_seq - 1, retreat, jnp.zeros((team * band, HD), F32))
        start_all(g, *b2)
        bin_[g, seq] = bcarry[g, seq]

    lax.fori_loop(SPLIT_B[-1], heads, back_part, 0)

    lax.fori_loop(1, n_head, head_sent, 0)
    for g in range(groups):
        for route in (f1, f2, b1):
            sent_all(g, *route)

    def back_states(g):
        def go(h, _):
            carry = get_bands(bin_, g, h)
            for b in reversed(range(blocks)):
                bheld[b, h] = carry.astype(BF16)
                if b:
                    carry = blocal[b, h] + passrow[b, pl.ds(h, 1), :] * carry
            return 0

        return go

    for g in range(groups):
        wait_all(g, *b2)
        lax.fori_loop(g * team, (g + 1) * team, back_states(g), 0, unroll=True)
    for g in range(groups):
        sent_all(g, *b2)


def finish(
    heads, blocks,
    gated_ref, ggrad_ref, qgrad_ref, kpart, vpart, keyed, vkeyed, bheld,
    gated_hbm, ggrad_hbm, qgrad_hbm, kgrad_hbm, vgrad_hbm,
    kout, vout, sems,
):
    first = [
        pltpu.make_async_copy(src, dst, sems.at[i, 0])
        for i, (src, dst) in enumerate(
            ((gated_ref, gated_hbm), (ggrad_ref, ggrad_hbm), (qgrad_ref, qgrad_hbm))
        )
    ]
    for copy in first:
        copy.start()

    def strip(i, p):
        src, dst = ((kout, kgrad_hbm), (vout, vgrad_hbm))[i]
        lanes = pl.ds(pl.multiple_of(p * TEAM * HD, HD), TEAM * HD)
        return pltpu.make_async_copy(src.at[:, lanes], dst.at[:, lanes], sems.at[3 + i, p])

    def go(p, _):
        for i in range(TEAM):
            h = p * TEAM + i
            lanes = pl.ds(pl.multiple_of(h * HD, HD), HD)
            for b in range(blocks):
                rows = pl.ds(b * BLOCK, BLOCK)
                state = bheld[b, h]
                kout[rows, lanes] = (kpart[h, rows, :] + mm(vkeyed[h, rows, :], state, NT)).astype(BF16)
                vout[rows, lanes] = (vpart[h, rows, :] + mm(keyed[h, rows, :], state)).astype(BF16)
        strip(0, p).start()
        strip(1, p).start()
        return 0

    lax.fori_loop(0, heads // TEAM, go, 0)
    for copy in first:
        copy.wait()

    def done(p, _):
        strip(0, p).wait()
        strip(1, p).wait()
        return 0

    lax.fori_loop(0, heads // TEAM, done, 0)


def solution(mesh):
    n_seq, n_head = mesh.shape["seq"], mesh.shape["head"]

    def body(queries, key_rows, value_rows, log_decay, doc_start, gate_input, norm_gain, out_grad):
        rows, width = queries.shape
        heads = width // HD
        blocks = rows // BLOCK
        team = heads // GROUPS
        band = HD // n_seq
        whole = pl.BlockSpec(memory_space=pltpu.VMEM)
        hbm = pl.BlockSpec(memory_space=pl.ANY)
        dma = pltpu.SemaphoreType.DMA
        big = lambda kind: pltpu.VMEM((heads, rows, HD), kind)
        states = pltpu.VMEM((GROUPS, n_seq, team * band, HD), F32)
        wide = pltpu.VMEM((GROUPS, n_seq, team * band + 8, HD), F32)
        seq_sems = dma((GROUPS, n_seq))
        outs = pl.pallas_call(
            functools.partial(kernel, n_seq, n_head, heads, blocks, GROUPS),
            name="lightning",
            out_shape=[pltpu.VMEM((rows, width), BF16)] * 3
            + [big(F32), big(F32), big(BF16), big(BF16), pltpu.VMEM((blocks, heads, HD, HD), BF16)],
            in_specs=[hbm] * 8,
            out_specs=[whole] * 8,
            scratch_shapes=[
                big(BF16), big(BF16), big(BF16), big(BF16), big(BF16), dma((5, heads)),
                pltpu.VMEM((heads, rows), F32),
                pltpu.VMEM((8, HD), jnp.int32),
                pltpu.VMEM((8, HD), F32),
                dma((3,)),
                pltpu.VMEM((blocks, heads, BLOCK), F32),
                pltpu.VMEM((blocks, heads, BLOCK), F32),
                pltpu.VMEM((blocks, heads, HD), F32),
                pltpu.VMEM((blocks, BLOCK, HD), BF16),
                pltpu.VMEM((blocks, BLOCK, BLOCK), F32),
                pltpu.VMEM((heads, blocks, 3, HALF, HALF), BF16),
                pltpu.VMEM((heads, blocks, 3, HALF, HALF), BF16),
                big(BF16),
                pltpu.VMEM((blocks, heads, HD, HD), F32),
                pltpu.VMEM((blocks, heads, HD, HD), F32),
                pltpu.VMEM((blocks, heads, HD, HD), BF16),
                pltpu.VMEM((2, rows, HD), F32),
                pltpu.VMEM((2, rows, HD), F32),
                wide, wide, states, states, states, states, states, states,
                pltpu.VMEM((n_head, 16, HD), F32),
                seq_sems, seq_sems, seq_sems, seq_sems, seq_sems, seq_sems, seq_sems, seq_sems,
                dma((n_head,)), dma((n_head,)),
            ],
            compiler_params=pltpu.CompilerParams(
                collective_id=0, has_side_effects=True, vmem_limit_bytes=38 << 20
            ),
        )(
            queries, key_rows, value_rows, gate_input, out_grad, log_decay,
            doc_start.reshape(8, HD), norm_gain.reshape(8, HD),
        )
        return tuple(
            pl.pallas_call(
                functools.partial(finish, heads, blocks),
                name="finish",
                out_shape=[jax.ShapeDtypeStruct((rows, width), BF16)] * 5,
                in_specs=[whole] * 8,
                out_specs=[hbm] * 5,
                scratch_shapes=[
                    pltpu.VMEM((rows, width), BF16),
                    pltpu.VMEM((rows, width), BF16),
                    dma((5, heads // TEAM)),
                ],
                compiler_params=pltpu.CompilerParams(vmem_limit_bytes=6 << 20),
            )(*[pltpu.with_memory_space_constraint(out, pltpu.VMEM) for out in outs])
        )

    block = P("seq", "head")
    return jax.shard_map(
        body,
        mesh=mesh,
        in_specs=(block, block, block, P("head", "seq"), P("seq"), block, P("head"), block),
        out_specs=(block,) * 5,
        check_vma=False,
    )
```

```python
import functools

import jax
import jax.numpy as jnp
from jax import lax
from jax.experimental import pallas as pl
from jax.experimental.pallas import tpu as pltpu
from jax.sharding import PartitionSpec as P

HEAD_TOTAL = 64
HD = 128
BLOCK = 512
HALF = 256
EPSILON = 1e-06
GROUPS = 2
SPLIT_F = (4, 4)
SPLIT_B = (3, 4)
UNROLL = True
TEAM = 2
MESH = pl.DeviceIdType.MESH
F32 = jnp.float32
BF16 = jnp.bfloat16

NN = (((1,), (0,)), ((), ()))
NT = (((1,), (1,)), ((), ()))
TN = (((0,), (0,)), ((), ()))

CUM, ENTER, LEAVE, COUNT = range(4)


def mm(a, b, dims=NN):
    return lax.dot_general(a, b, dims, preferred_element_type=F32)


def pieces(x):
    hi = x.astype(BF16).astype(F32)
    rest = x - hi
    mid = rest.astype(BF16).astype(F32)
    low = (rest - mid).astype(BF16).astype(F32)
    return hi, mid, low


def running_sum(x):
    lane = lax.broadcasted_iota(jnp.int32, x.shape, 1)
    shift = 1
    while shift < x.shape[1]:
        x = x + jnp.where(lane >= shift, pltpu.roll(x, shift, 1), 0.0)
        shift *= 2
    return x


def kernel(
    n_seq, n_head, heads, blocks, groups,
    q_hbm, k_hbm, v_hbm, gate_hbm, og_hbm, decay_hbm, doc_hbm, gain_hbm,
    gated_ref, ggrad_ref, qgrad_ref, attn, gbuf, keyed, qkeyed, bheld,
    qb, kb, vb, gateb, ogb, in_sem, decay_ref, doc_ref, gain_ref, small_sem,
    crow, leave_rows, passrow, cols, mask, wbuf, pbuf, agrad,
    local, blocal, held, acc, norm,
    fsend, frecv, fcarry, fin, bsend, brecv, bcarry, bin_, sums,
    f1s, f1r, f2s, f2r, b1s, b1r, b2s, b2r, hs, hr,
):
    seq = lax.axis_index("seq")
    hx = lax.axis_index("head")
    width = HEAD_TOTAL * HD
    team = heads // groups
    band = HD // n_seq

    barrier = pltpu.get_barrier_semaphore()

    def greet_seq(o, _):
        pl.semaphore_signal(barrier, inc=1, device_id={"seq": lax.rem(seq + o, n_seq)}, device_id_type=MESH)
        return 0

    def greet_head(o, _):
        pl.semaphore_signal(barrier, inc=1, device_id={"head": lax.rem(hx + o, n_head)}, device_id_type=MESH)
        return 0

    small = [
        pltpu.make_async_copy(src, dst, small_sem.at[i])
        for i, (src, dst) in enumerate(((decay_hbm, decay_ref), (doc_hbm, doc_ref), (gain_hbm, gain_ref)))
    ]
    for copy in small:
        copy.start()
    pairs = ((k_hbm, kb), (v_hbm, vb), (q_hbm, qb), (gate_hbm, gateb), (og_hbm, ogb))

    def load(i, h):
        src, dst = pairs[i]
        return pltpu.make_async_copy(
            src.at[:, pl.ds(pl.multiple_of(h * HD, HD), HD)], dst.at[h], in_sem.at[i, h]
        )

    def start_kv(h, _):
        load(0, h).start()
        load(1, h).start()
        return 0

    def start_rest(i):
        def go(h, _):
            load(i, h).start()
            return 0

        return go

    lax.fori_loop(0, heads, start_kv, 0)
    lax.fori_loop(1, n_seq, greet_seq, 0)
    lax.fori_loop(1, n_head, greet_head, 0)
    for copy in small:
        copy.wait()

    doc = doc_ref[...].astype(F32)
    per = BLOCK // HD
    total = None
    for b in range(blocks):
        flags = jnp.concatenate([doc[b * per + i : b * per + i + 1, :] for i in range(per)], axis=1)
        flags = jnp.broadcast_to(flags, (heads, BLOCK))
        c = running_sum(decay_ref[:, b * BLOCK : (b + 1) * BLOCK])
        r = running_sum(flags)
        c_last = c[:, BLOCK - 1 :]
        r_last = r[:, BLOCK - 1 :]
        enter = jnp.where(r == 0.0, jnp.exp(c), 0.0)
        leave = jnp.where(r == r_last, jnp.exp(c_last - c), 0.0)
        passing = jnp.where(r_last == 0.0, jnp.exp(c_last), 0.0)
        passing = jnp.broadcast_to(passing, (heads, HD))
        crow[b] = c
        leave_rows[b] = leave
        passrow[b] = passing
        total = passing if total is None else total * passing
        hi, mid, low = pieces(jnp.concatenate([c, enter, leave, r], axis=0))
        stacked = jnp.concatenate([hi, mid, low, jnp.zeros_like(hi)], axis=0)
        cols[b] = stacked.T.astype(BF16)
    tail = team * band
    fsend[0, :, tail : tail + 8, :] = jnp.broadcast_to(total[None], (n_seq, heads, HD))
    lax.fori_loop(0, heads, start_rest(2), 0)

    def pick(h, *quantities):
        row = lax.broadcasted_iota(jnp.int32, (HD, HD), 0)
        live = row < 96
        out = [
            jnp.where(live & ((row & 31) == quantity * 8 + h), 1.0, 0.0).astype(BF16)
            for quantity in quantities
        ]
        return jnp.concatenate(out, axis=1) if len(out) > 1 else out[0]

    def columns(b, h, *quantities):
        both = mm(cols[b], pick(h, *quantities))
        return [both[:, i * HD : (i + 1) * HD] for i in range(len(quantities))]

    def exchange(g, src, dst, s_sem, r_sem, o):
        peer = lax.rem(seq + 5 * o, n_seq)
        part = pl.ds(0, tail + 8 if src is fsend and g == 0 else tail)
        return pltpu.make_async_remote_copy(
            src_ref=src.at[g, peer, part], dst_ref=dst.at[g, seq, part], send_sem=s_sem.at[g, o], recv_sem=r_sem.at[g, o],
            device_id={"seq": peer}, device_id_type=MESH,
        )

    def start_all(g, src, dst, s_sem, r_sem):
        def go(o, _):
            exchange(g, src, dst, s_sem, r_sem, o).start()
            return 0

        lax.fori_loop(1, n_seq, go, 0, unroll=UNROLL)

    def wait_all(g, src, dst, s_sem, r_sem):
        def go(o, _):
            exchange(g, src, dst, s_sem, r_sem, o).wait_recv()
            return 0

        lax.fori_loop(1, n_seq, go, 0, unroll=UNROLL)

    def sent_all(g, src, dst, s_sem, r_sem):
        def go(o, _):
            exchange(g, src, dst, s_sem, r_sem, o).wait_send()
            return 0

        lax.fori_loop(1, n_seq, go, 0)

    def put_bands(ref, g, h, state):
        place = pl.ds(pl.multiple_of((h - g * team) * band, band), band)
        ref[g, :, place, :] = state.reshape(n_seq, band, HD)

    def get_bands(ref, g, h):
        place = pl.ds(pl.multiple_of((h - g * team) * band, band), band)
        return ref[g, :, place, :].reshape(HD, HD)

    def pass_bands(d, g):
        return jnp.concatenate(
            [jnp.broadcast_to(frecv[0, d, tail + g * team + i : tail + g * team + i + 1, :], (band, HD)) for i in range(team)],
            axis=0,
        )

    f1 = (fsend, frecv, f1s, f1r)
    f2 = (fcarry, fin, f2s, f2r)
    b1 = (bsend, brecv, b1s, b1r)
    b2 = (bcarry, bin_, b2s, b2r)

    def local_states(g):
        def go(h, _):
            load(0, h).wait()
            load(1, h).wait()
            state = None
            for b in range(blocks):
                rows = pl.ds(b * BLOCK, BLOCK)
                key_t = kb[h, rows, :].T.astype(F32) * leave_rows[b, pl.ds(h, 1), :]
                part = mm(key_t.astype(BF16), vb[h, rows, :])
                local[b, h] = part
                state = part if state is None else passrow[b, pl.ds(h, 1), :] * state + part
            put_bands(fsend, g, h, state)
            return 0

        return go

    for g in range(groups):
        lax.fori_loop(g * team, (g + 1) * team, local_states(g), 0, unroll=4)
        if g == 0:
            pl.semaphore_wait(barrier, n_seq - 1 + n_head - 1)
        start_all(g, *f1)
    lax.fori_loop(0, heads, start_rest(3), 0)
    lax.fori_loop(0, heads, start_rest(4), 0)

    for b in range(blocks):
        (r_col,) = columns(b, 0, COUNT)
        flags = jnp.concatenate([doc[b * per + i : b * per + i + 1, :] for i in range(per)], axis=1)
        r_row = running_sum(jnp.broadcast_to(flags, (8, BLOCK)))[0:1, :]
        for i in range(BLOCK // HD):
            t = lax.broadcasted_iota(jnp.int32, (BLOCK, HD), 0)
            j = lax.broadcasted_iota(jnp.int32, (BLOCK, HD), 1) + i * HD
            same = r_col == r_row[:, i * HD : (i + 1) * HD]
            mask[b, :, i * HD : (i + 1) * HD] = jnp.where(same & (j <= t), jnp.inf, -jnp.inf)

    tiles = [(0, 0), (1, 0), (1, 1)]
    qkeyed_t = keyed

    def inside_part(h, _):
        load(2, h).wait()
        for b in range(blocks):
            rows = pl.ds(b * BLOCK, BLOCK)
            cum, enter = columns(b, h, CUM, ENTER)
            query = qb[h, rows, :]
            scaled = (query.astype(F32) * enter).astype(BF16)
            qkeyed[h, rows, :] = scaled
            turned = scaled.T
            for i in range(BLOCK // HD):
                qkeyed_t[h, pl.ds(b * BLOCK + i * HD, HD), :] = turned[:, i * HD : (i + 1) * HD]
            row = crow[b, pl.ds(h, 1), :]
            out = [None, None]
            for index, (ti, tj) in enumerate(tiles):
                t = slice(ti * HALF, (ti + 1) * HALF)
                j = slice(tj * HALF, (tj + 1) * HALF)
                score = mm(query[t], kb[h, pl.ds(b * BLOCK + tj * HALF, HALF), :], NT)
                c_t = cum[t]
                diff = jnp.concatenate([c_t, c_t], axis=1) - row[:, j]
                w = jnp.exp(jnp.minimum(diff, mask[b, t, j]))
                prob = (score * w).astype(BF16)
                wbuf[h, b, index] = w.astype(BF16)
                pbuf[h, b, index] = prob
                part = mm(prob, vb[h, pl.ds(b * BLOCK + tj * HALF, HALF), :])
                out[ti] = part if out[ti] is None else out[ti] + part
            for ti in range(2):
                attn[h, pl.ds(b * BLOCK + ti * HALF, HALF), :] = out[ti]
        return 0

    lax.fori_loop(0, SPLIT_F[0], inside_part, 0)
    for g in range(groups):
        if g:
            lax.fori_loop(SPLIT_F[g - 1], SPLIT_F[g], inside_part, 0)
        wait_all(g, *f1)
        mine = pl.ds(0, tail + 8 if g == 0 else tail)
        frecv[g, seq, mine] = fsend[g, seq, mine]
        fcarry[g, 0] = jnp.zeros((team * band, HD), F32)

        def advance(d, carry):
            carry = pass_bands(d, g) * carry + frecv[g, d, 0:tail]
            fcarry[g, d + 1] = carry
            return carry

        lax.fori_loop(0, n_seq - 1, advance, jnp.zeros((team * band, HD), F32), unroll=UNROLL)
        start_all(g, *f2)
        fin[g, seq] = fcarry[g, seq]

    lax.fori_loop(SPLIT_F[-1], heads, inside_part, 0)

    def gate_part(h, _):
        load(3, h).wait()
        load(4, h).wait()
        sig = jax.nn.sigmoid(gateb[h].astype(F32))
        gbuf[h] = ogb[h].astype(F32) * sig * gain_ref[pl.ds(h, 1), :]
        return 0

    lax.fori_loop(0, heads, gate_part, 0)
    acc[...] = jnp.zeros_like(acc)

    def outside_part(g):
        def go(h, _):
            carry = get_bands(fin, g, h)
            for b in range(blocks):
                rows = pl.ds(b * BLOCK, BLOCK)
                state = carry.astype(BF16)
                held[b, h] = state
                out = attn[h, rows, :] + mm(qkeyed[h, rows, :], state)
                attn[h, rows, :] = out
                acc[0, rows, :] += out * out
                acc[1, rows, :] += out * gbuf[h, rows, :]
                if b + 1 < blocks:
                    carry = passrow[b, pl.ds(h, 1), :] * carry + local[b, h]
            return 0

        return go

    for g in range(groups):
        wait_all(g, *f2)
        lax.fori_loop(g * team, (g + 1) * team, outside_part(g), 0, unroll=4)

    parts = []
    for i in range(2):
        value = acc[i]
        hi = value.astype(BF16)
        parts += [hi, (value - hi.astype(F32)).astype(BF16)]
    row = lax.broadcasted_iota(jnp.int32, (8, 4 * HD), 0)
    lane = lax.broadcasted_iota(jnp.int32, (8, 4 * HD), 1)
    chooser = jnp.where((row < 4) == (lane < 2 * HD), 1.0, 0.0).astype(BF16)
    totals = mm(chooser, jnp.concatenate(parts, axis=1), NT)
    pieces_n = totals.shape[1] // HD
    sums[hx] = jnp.concatenate(
        [totals[r : r + 1, i * HD : (i + 1) * HD] for r in (0, 4) for i in range(pieces_n)], axis=0
    )

    def head_copy(o):
        peer = lax.rem(hx + o, n_head)
        return pltpu.make_async_remote_copy(
            src_ref=sums.at[hx], dst_ref=sums.at[hx], send_sem=hs.at[o], recv_sem=hr.at[o],
            device_id={"head": peer}, device_id_type=MESH,
        )

    def head_start(o, _):
        head_copy(o).start()
        return 0

    def head_wait(o, _):
        head_copy(o).wait_recv()
        return 0

    def head_sent(o, _):
        head_copy(o).wait_send()
        return 0

    lax.fori_loop(1, n_head, head_start, 0, unroll=UNROLL)
    lax.fori_loop(1, n_head, head_wait, 0, unroll=UNROLL)
    both = sums[0]
    for i in range(1, n_head):
        both = both + sums[i]
    inverse = lax.rsqrt(both[0:8, :] / width + EPSILON)
    coef = inverse * inverse * inverse * both[8:16, :] / width
    hi, mid, low = pieces(jnp.concatenate([inverse, coef, jnp.zeros((16, HD), F32)], axis=0))
    turned = jnp.concatenate([hi, mid, low, jnp.zeros_like(hi)], axis=0).T.astype(BF16)
    for i in range(8):
        wide = mm(turned, pick(i, 0, 1))
        norm[0, i * HD : (i + 1) * HD, :] = wide[:, :HD]
        norm[1, i * HD : (i + 1) * HD, :] = wide[:, HD:]

    def grad_part(g):
        def go(h, _):
            state = None
            for b in reversed(range(blocks)):
                rows = pl.ds(b * BLOCK, BLOCK)
                ag = (norm[0, rows, :] * gbuf[h, rows, :] - attn[h, rows, :] * norm[1, rows, :]).astype(BF16)
                agrad[h, rows, :] = ag
                turned = [qkeyed_t[h, pl.ds(b * BLOCK + i * HD, HD), :] for i in range(BLOCK // HD)]
                part = mm(jnp.concatenate(turned, axis=1), ag)
                blocal[b, h] = part
                state = part if state is None else part + passrow[b, pl.ds(h, 1), :] * state
            put_bands(bsend, g, h, state)
            return 0

        return go

    for g in range(groups):
        lax.fori_loop(g * team, (g + 1) * team, grad_part(g), 0, unroll=4)
        start_all(g, *b1)

    vkeyed = qkeyed

    def back_part(h, _):
        lanes = pl.ds(pl.multiple_of(h * HD, HD), HD)
        gain = gain_ref[pl.ds(h, 1), :]
        sig = jax.nn.sigmoid(gateb[h].astype(F32))
        gate = attn[h] * norm[0] * gain * sig
        gated_ref[:, lanes] = gate.astype(BF16)
        ggrad_ref[:, lanes] = (ogb[h].astype(F32) * gate * (1.0 - sig)).astype(BF16)
        for b in range(blocks):
            rows = pl.ds(b * BLOCK, BLOCK)
            enter, leave = columns(b, h, ENTER, LEAVE)
            query = qb[h, rows, :]
            key = kb[h, rows, :]
            value = vb[h, rows, :]
            keyed[h, rows, :] = (key.astype(F32) * leave).astype(BF16)
            vkeyed[h, rows, :] = (value.astype(F32) * leave).astype(BF16)
            ag = agrad[h, rows, :]
            query_t, ag_t = query.T, ag.T
            qg = [None, None]
            kg = [None, None]
            vg = [None, None]
            for index, (ti, tj) in enumerate(tiles):
                t = slice(ti * HALF, (ti + 1) * HALF)
                j = slice(tj * HALF, (tj + 1) * HALF)
                ds = (mm(ag[t], value[j], NT) * wbuf[h, b, index].astype(F32)).astype(BF16)
                part = mm(ds, key[j])
                qg[ti] = part if qg[ti] is None else qg[ti] + part
                part = mm(query_t[:, t], ds)
                kg[tj] = part if kg[tj] is None else kg[tj] + part
                part = mm(ag_t[:, t], pbuf[h, b, index])
                vg[tj] = part if vg[tj] is None else vg[tj] + part
            outside = mm(ag, held[b, h], NT) * enter
            for i in range(2):
                here = pl.ds(b * BLOCK + i * HALF, HALF)
                qgrad_ref[here, lanes] = (qg[i] + outside[i * HALF : (i + 1) * HALF]).astype(BF16)
                attn[h, here, :] = kg[i].T
                gbuf[h, here, :] = vg[i].T
        return 0

    lax.fori_loop(0, SPLIT_B[0], back_part, 0)
    for g in range(groups):
        if g:
            lax.fori_loop(SPLIT_B[g - 1], SPLIT_B[g], back_part, 0)
        wait_all(g, *b1)
        brecv[g, seq] = bsend[g, seq]
        bcarry[g, n_seq - 1] = jnp.zeros((team * band, HD), F32)

        def retreat(i, carry):
            d = n_seq - 1 - i
            carry = pass_bands(d, g) * carry + brecv[g, d]
            bcarry[g, d - 1] = carry
            return carry

        lax.fori_loop(0, n_seq - 1, retreat, jnp.zeros((team * band, HD), F32), unroll=UNROLL)
        start_all(g, *b2)
        bin_[g, seq] = bcarry[g, seq]

    lax.fori_loop(SPLIT_B[-1], heads, back_part, 0)

    lax.fori_loop(1, n_head, head_sent, 0)
    for g in range(groups):
        for route in (f1, f2, b1):
            sent_all(g, *route)

    def back_states(g):
        def go(h, _):
            carry = get_bands(bin_, g, h)
            for b in reversed(range(blocks)):
                bheld[b, h] = carry.astype(BF16)
                if b:
                    carry = blocal[b, h] + passrow[b, pl.ds(h, 1), :] * carry
            return 0

        return go

    for g in range(groups):
        wait_all(g, *b2)
        lax.fori_loop(g * team, (g + 1) * team, back_states(g), 0, unroll=True)
    for g in range(groups):
        sent_all(g, *b2)


def finish(
    heads, blocks,
    gated_ref, ggrad_ref, qgrad_ref, kpart, vpart, keyed, vkeyed, bheld,
    gated_hbm, ggrad_hbm, qgrad_hbm, kgrad_hbm, vgrad_hbm,
    kout, vout, sems,
):
    first = [
        pltpu.make_async_copy(src, dst, sems.at[i, 0])
        for i, (src, dst) in enumerate(
            ((gated_ref, gated_hbm), (ggrad_ref, ggrad_hbm), (qgrad_ref, qgrad_hbm))
        )
    ]
    for copy in first:
        copy.start()

    def strip(i, p):
        src, dst = ((kout, kgrad_hbm), (vout, vgrad_hbm))[i]
        lanes = pl.ds(pl.multiple_of(p * TEAM * HD, HD), TEAM * HD)
        return pltpu.make_async_copy(src.at[:, lanes], dst.at[:, lanes], sems.at[3 + i, p])

    def go(p, _):
        for i in range(TEAM):
            h = p * TEAM + i
            lanes = pl.ds(pl.multiple_of(h * HD, HD), HD)
            for b in range(blocks):
                rows = pl.ds(b * BLOCK, BLOCK)
                state = bheld[b, h]
                kout[rows, lanes] = (kpart[h, rows, :] + mm(vkeyed[h, rows, :], state, NT)).astype(BF16)
                vout[rows, lanes] = (vpart[h, rows, :] + mm(keyed[h, rows, :], state)).astype(BF16)
        strip(0, p).start()
        strip(1, p).start()
        return 0

    lax.fori_loop(0, heads // TEAM, go, 0)
    for copy in first:
        copy.wait()

    def done(p, _):
        strip(0, p).wait()
        strip(1, p).wait()
        return 0

    lax.fori_loop(0, heads // TEAM, done, 0)


def solution(mesh):
    n_seq, n_head = mesh.shape["seq"], mesh.shape["head"]

    def body(queries, key_rows, value_rows, log_decay, doc_start, gate_input, norm_gain, out_grad):
        rows, width = queries.shape
        heads = width // HD
        blocks = rows // BLOCK
        team = heads // GROUPS
        band = HD // n_seq
        whole = pl.BlockSpec(memory_space=pltpu.VMEM)
        hbm = pl.BlockSpec(memory_space=pl.ANY)
        dma = pltpu.SemaphoreType.DMA
        big = lambda kind: pltpu.VMEM((heads, rows, HD), kind)
        states = pltpu.VMEM((GROUPS, n_seq, team * band, HD), F32)
        wide = pltpu.VMEM((GROUPS, n_seq, team * band + 8, HD), F32)
        seq_sems = dma((GROUPS, n_seq))
        outs = pl.pallas_call(
            functools.partial(kernel, n_seq, n_head, heads, blocks, GROUPS),
            name="lightning",
            out_shape=[pltpu.VMEM((rows, width), BF16)] * 3
            + [big(F32), big(F32), big(BF16), big(BF16), pltpu.VMEM((blocks, heads, HD, HD), BF16)],
            in_specs=[hbm] * 8,
            out_specs=[whole] * 8,
            scratch_shapes=[
                big(BF16), big(BF16), big(BF16), big(BF16), big(BF16), dma((5, heads)),
                pltpu.VMEM((heads, rows), F32),
                pltpu.VMEM((8, HD), jnp.int32),
                pltpu.VMEM((8, HD), F32),
                dma((3,)),
                pltpu.VMEM((blocks, heads, BLOCK), F32),
                pltpu.VMEM((blocks, heads, BLOCK), F32),
                pltpu.VMEM((blocks, heads, HD), F32),
                pltpu.VMEM((blocks, BLOCK, HD), BF16),
                pltpu.VMEM((blocks, BLOCK, BLOCK), F32),
                pltpu.VMEM((heads, blocks, 3, HALF, HALF), BF16),
                pltpu.VMEM((heads, blocks, 3, HALF, HALF), BF16),
                big(BF16),
                pltpu.VMEM((blocks, heads, HD, HD), F32),
                pltpu.VMEM((blocks, heads, HD, HD), F32),
                pltpu.VMEM((blocks, heads, HD, HD), BF16),
                pltpu.VMEM((2, rows, HD), F32),
                pltpu.VMEM((2, rows, HD), F32),
                wide, wide, states, states, states, states, states, states,
                pltpu.VMEM((n_head, 16, HD), F32),
                seq_sems, seq_sems, seq_sems, seq_sems, seq_sems, seq_sems, seq_sems, seq_sems,
                dma((n_head,)), dma((n_head,)),
            ],
            compiler_params=pltpu.CompilerParams(
                collective_id=0, has_side_effects=True, vmem_limit_bytes=38 << 20
            ),
        )(
            queries, key_rows, value_rows, gate_input, out_grad, log_decay,
            doc_start.reshape(8, HD), norm_gain.reshape(8, HD),
        )
        return tuple(
            pl.pallas_call(
                functools.partial(finish, heads, blocks),
                name="finish",
                out_shape=[jax.ShapeDtypeStruct((rows, width), BF16)] * 5,
                in_specs=[whole] * 8,
                out_specs=[hbm] * 5,
                scratch_shapes=[
                    pltpu.VMEM((rows, width), BF16),
                    pltpu.VMEM((rows, width), BF16),
                    dma((5, heads // TEAM)),
                ],
                compiler_params=pltpu.CompilerParams(vmem_limit_bytes=6 << 20),
            )(*[pltpu.with_memory_space_constraint(out, pltpu.VMEM) for out in outs])
        )

    block = P("seq", "head")
    return jax.shard_map(
        body,
        mesh=mesh,
        in_specs=(block, block, block, P("head", "seq"), P("seq"), block, P("head"), block),
        out_specs=(block,) * 5,
        check_vma=False,
    )
```
